32 devices in a mesh: dp: 16 (over z, x, core), tensor: 2 (over y).
Axes of the slice: x: 2, y: 2, z: 4, core: 2. Of those that a mesh axis runs over, the one named last changes fastest.
Arguments:
- inputs: bfloat16 [32, 256, 512], P('dp'), may hold values from -6 to 6
- cotangent: bfloat16 [32, 256, 512], P('dp'), may hold values from -6 to 6
- group_ids: int32 [32], P('dp'), may hold values from 0 to 2
- group_weights: int32 [3], replicated, may hold values from 1 to 4
- filters: bfloat16 [256, 24], replicated, may hold values from -0.375 to 0.375
- gain_mixer: float32 [512], replicated, may hold values from 0.5 to 1.5
- mixer_weights: bfloat16 [2, 24, 512, 512], P(None, 'tensor'), may hold values from -0.0390625 to 0.0390625
- ar_weights: bfloat16 [3, 512, 512], replicated, may hold values from -0.15625 to 0.15625
- gain_mlp: float32 [512], replicated, may hold values from 0.5 to 1.5
- w_gate: bfloat16 [512, 2048], P(None, 'tensor'), may hold values from -0.25 to 0.25
- w_up: bfloat16 [512, 2048], P(None, 'tensor'), may hold values from -0.25 to 0.25
- w_down: bfloat16 [2048, 512], P('tensor'), may hold values from -0.125 to 0.125
Outputs:
- output: float32 [32, 256, 512], P('dp')
- input_grad: float32 [32, 256, 512], P('dp')
- grad_gain_mixer: float32 [512], P('dp')
- grad_mixer: float32 [2, 24, 512, 512], P(None, 'tensor', 'dp')
- grad_ar: float32 [3, 512, 512], P(None, 'dp')
- grad_gain_mlp: float32 [512], P('dp')
- grad_gate: float32 [512, 2048], P('dp', 'tensor')
- grad_up: float32 [512, 2048], P('dp', 'tensor')
- grad_down: float32 [2048, 512], P('tensor', 'dp')
The draws below stay inside these ranges and needn't reach their ends.
All inputs are finite; a program needn't handle non-finite values.
Results may differ from the reference program's by a relative error of at most 0.02.
Values may be sent and summed in bfloat16 or wider, within the bound.
A program may use at most 256 MiB of HBM per device.

```python
import math
import jax
import jax.numpy as jnp
import numpy as np
from jax import lax

D = 512
K = 24
FF = 2048
ORDER = 3
GROUPS = 3
LEN = 256
SEQS = 32


def set_ends(drawn, key, smallest, high):
    dims = drawn.shape
    index_at = [jax.random.randint(jax.random.fold_in(key, axis), (), 0, dims[axis]) for axis in range(len(dims))]
    drawn = drawn.at[tuple(index_at)].set(smallest)
    longest = dims.index(max(dims))
    index_at[longest] = (index_at[longest] + 1) % dims[longest]
    return drawn.at[tuple(index_at)].set(high)


def block_levels(rng, shape, split, least, high):
    factor_of, own = 1.0, jax.random.fold_in(rng, 6)
    for position, blocks in split:
        draws = jnp.exp(jax.random.uniform(jax.random.fold_in(own, position), (blocks,), jnp.float32, least / len(split), high / len(split)))
        factor_of = factor_of * jnp.repeat(draws, shape[position] // blocks).reshape([-1 if axis == position else 1 for axis in range(len(shape))])
    return factor_of


def rank_bounds(number_of, skew):
    weights = [(1 << 20) // math.isqrt(grade ** skew) + 1 for grade in range(1, number_of + 1)]
    deviation = 1 + sum(weights) // (1 << 30)
    return np.cumsum(np.array([max(1, weight // deviation) for weight in weights]))


def ranked(rng, dims, amount, skew):
    table = rank_bounds(amount, skew)
    pick = jax.random.randint(jax.random.fold_in(rng, 1), dims, 0, int(table[amount - 1]))
    standing = jnp.searchsorted(jnp.asarray(table, jnp.int32), pick, side="right")
    return jax.random.permutation(jax.random.fold_in(rng, 2), amount)[standing].astype(jnp.int32)


def bell_draw(stream_key, dims, scale, most, shards=(), held_as=jnp.bfloat16):
    level = block_levels(stream_key, dims, shards, -0.22, 0.18) if shards else 1.0
    drawn = jax.random.normal(stream_key, dims, jnp.float32) * scale * level
    return jnp.minimum(jnp.maximum(drawn, -most), most).astype(held_as)


def setup_inputs(seed: int = 0) -> dict:
    key_list = jax.random.split(jax.random.key(seed), 13)
    return {
        "inputs": bell_draw(key_list[0], (SEQS, LEN, D), 1.0, 6.0, ((0, 16),)),
        "cotangent": bell_draw(key_list[1], (SEQS, LEN, D), 1.0, 6.0, ((0, 16),)),
        "group_ids": set_ends(ranked(key_list[2], (SEQS,), GROUPS, 2), jax.random.fold_in(key_list[2], 3), 0, GROUPS - 1).astype(jnp.int32),
        "group_weights": jax.random.randint(key_list[3], (GROUPS,), 1, 5).astype(jnp.int32),
        "filters": bell_draw(key_list[4], (LEN, K), LEN ** -0.5, 0.375),
        "gain_mixer": jnp.clip(1.0 + 0.1 * jax.random.normal(key_list[5], (D,), jnp.float32), 0.5, 1.5),
        "mixer_weights": bell_draw(key_list[6], (2, K, D, D), (2 * K * D) ** -0.5, 0.0390625, ((1, 2),)),
        "ar_weights": bell_draw(key_list[7], (ORDER, D, D), (ORDER * D) ** -0.5, 0.15625),
        "gain_mlp": jnp.clip(1.0 + 0.1 * jax.random.normal(key_list[8], (D,), jnp.float32), 0.5, 1.5),
        "w_gate": bell_draw(key_list[9], (D, FF), D ** -0.5, 0.25, ((1, 2),)),
        "w_up": bell_draw(key_list[10], (D, FF), D ** -0.5, 0.25, ((1, 2),)),
        "w_down": bell_draw(key_list[11], (FF, D), FF ** -0.5, 0.125, ((0, 2),)),
    }


@jax.custom_vjp
def low(v):
    return lax.optimization_barrier(v.astype(jnp.bfloat16)).astype(jnp.float32)

@jax.custom_vjp
def low_back(v):
    return v

def low_keep(v):
    return (low(v), None)

def low_pass(kept, grad):
    return (grad,)

def back_keep(v):
    return (v, None)

def back_low(kept, grad):
    return (low(grad),)
low.defvjp(low_keep, low_pass)
low_back.defvjp(back_keep, back_low)
EPSILON = 1e-06

def rms_scale(values):
    return lax.rsqrt(lax.optimization_barrier(jnp.mean(values * values, axis=-1, keepdims=True)) + EPSILON)

def dense_product(left_side, right_side):
    return jnp.dot(left_side, right_side, precision=lax.Precision.HIGHEST, preferred_element_type=jnp.float32)

def gelu_exact(values):
    return 0.5 * values * (1.0 + jax.scipy.special.erf(values * 0.7071067811865476))

def stu_block(sequence, filters_both, gain_mixer, mixer_weights, ar_weights, gain_mlp, w_gate, w_up, w_down):
    length = sequence.shape[0]
    model_width = sequence.shape[1]
    normed = low(sequence * rms_scale(sequence) * gain_mixer)
    spectrum = jnp.fft.rfft(normed, n=2 * length, axis=0)
    filter_spec = jnp.fft.rfft(filters_both, n=2 * length, axis=0)
    conv_out = jnp.fft.irfft(filter_spec[:, :, None] * spectrum[:, None, :], n=2 * length, axis=0)[:length]
    conv_out = low(low_back(conv_out))
    filter_count = filters_both.shape[1]
    mixer_out = dense_product(conv_out.reshape(length, filter_count * model_width), mixer_weights.reshape(filter_count * model_width, model_width))
    lagged = jnp.concatenate([jnp.pad(normed, ((offset, 0), (0, 0)))[:length] for offset in range(ORDER)], axis=1)
    mixer_out = mixer_out + dense_product(lagged, ar_weights.reshape(ORDER * model_width, model_width))
    hidden_in = sequence + low_back(mixer_out)
    normed_two = low(hidden_in * rms_scale(hidden_in) * gain_mlp)
    gate_proj = low_back(dense_product(normed_two, w_gate))
    up_proj = low_back(dense_product(normed_two, w_up))
    active = low(gelu_exact(gate_proj) * up_proj)
    return hidden_in + low_back(dense_product(active, w_down))

def reference(inputs, cotangent, group_ids, group_weights, filters, gain_mixer, mixer_weights, ar_weights, gain_mlp, w_gate, w_up, w_down):
    filter_cols = filters.astype(jnp.float32)
    parity = 1.0 - 2.0 * (jnp.arange(LEN, dtype=jnp.int32) % 2).astype(jnp.float32)
    filters_both = jnp.concatenate([filter_cols, filter_cols * parity[:, None]], axis=1)

    def forward(x_all, gain_one, mixer_all, ar_all, gain_two, gate_all, up_all, down_all):

        def single(sequence):
            return stu_block(sequence, filters_both, gain_one, mixer_all, ar_all, gain_two, gate_all, up_all, down_all)
        return lax.map(jax.checkpoint(single), x_all)
    primals = (inputs.astype(jnp.float32), gain_mixer.astype(jnp.float32), mixer_weights.astype(jnp.float32), ar_weights.astype(jnp.float32), gain_mlp.astype(jnp.float32), w_gate.astype(jnp.float32), w_up.astype(jnp.float32), w_down.astype(jnp.float32))
    output, pullback = jax.vjp(forward, *primals)
    member = (group_ids[:, None] == jnp.arange(GROUPS, dtype=jnp.int32)[None, :]).astype(jnp.float32)
    seq_scale = lax.optimization_barrier(jnp.sum(member * group_weights.astype(jnp.float32)[None, :], axis=1))
    grad_pieces = pullback(cotangent.astype(jnp.float32) * seq_scale[:, None, None])
    return (output, grad_pieces[0], grad_pieces[1], grad_pieces[2], grad_pieces[3], grad_pieces[4], grad_pieces[5], grad_pieces[6], grad_pieces[7])
```

```python
import functools

import jax
import jax.numpy as jnp
from jax import lax
from jax.experimental import pallas as pl
from jax.experimental.pallas import tpu as pltpu
from jax.sharding import PartitionSpec as P

F32 = jnp.float32
BF16 = jnp.bfloat16
MESH = pl.DeviceIdType.MESH
EPSILON = 1e-06
ROOT_HALF = 0.7071067811865476
INV_ROOT_TWO_PI = 0.3989422804014327
ORDER = 3
MIB = 2**20


def dot(left, right):
    return jnp.dot(left, right, preferred_element_type=F32)


def dot_cols(left, right):
    return lax.dot_general(left, right, (((1,), (1,)), ((), ())), preferred_element_type=F32)


def dot_rows(left, right):
    return lax.dot_general(left, right, (((0,), (0,)), ((), ())), preferred_element_type=F32)


def rms_scale(values):
    return lax.rsqrt(jnp.mean(values * values, axis=-1, keepdims=True) + EPSILON)


def row_sign(rows):
    odd = lax.broadcasted_iota(jnp.int32, (rows, 1), 0) % 2
    return 1.0 - 2.0 * odd.astype(F32)


def lane_sign(lanes):
    odd = lax.broadcasted_iota(jnp.int32, (1, lanes), 1) % 2
    return 1.0 - 2.0 * odd.astype(F32)


def aligned(index, step):
    return pl.ds(pl.multiple_of(index * step, step), step)


class Sizes:
    def __init__(self, mesh_shape, inputs, mixer_weights, filters, w_gate):
        self.seqs, self.length, self.width = inputs
        self.rows = self.seqs * self.length
        self.dp = mesh_shape["dp"]
        self.tensor = mesh_shape["tensor"]
        self.line = self.dp // 4
        self.own = mixer_weights[1]
        self.filters = filters[1]
        self.hidden = w_gate[1]
        self.slice = self.width // self.dp
        self.group = max(g for g in range(1, 5) if self.own % g == 0)
        self.half = self.width // 2


def place(z):
    dp = lax.axis_index("dp")
    return dp // 4, (dp // 2) % 2, dp % 2, lax.axis_index("tensor")


def dp_of(line, side, core):
    return (line * 2 + side) * 2 + core


def filter_rows(filters_ref, reverse):
    length = filters_ref.shape[0]
    source = lax.broadcasted_iota(jnp.int32, (length, length), 0)
    target = lax.broadcasted_iota(jnp.int32, (length, length), 1)
    if reverse:
        target = (length + length // 2 - target) % length
    pick = (source == target).astype(BF16)
    return dot_rows(filters_ref[...], pick)


def toeplitz_own(z, own_first, rows_ref, out_ref):
    length, half = z.length, z.length // 2
    lane = lax.broadcasted_iota(jnp.int32, (half, length), 1)
    row = lax.broadcasted_iota(jnp.int32, (half, length), 0)

    def step(k, carry):
        values = jnp.broadcast_to(rows_ref[pl.ds(own_first + k, 1), :], (half, length))
        rolled = pltpu.roll(values, 0, 1, stride=1, stride_axis=0)
        lower = jnp.where(lane <= row + half, rolled, 0.0).astype(BF16)
        out_ref[k, half:, :] = lower
        out_ref[k, :half, :half] = lower[:, half:]
        out_ref[k, :half, half:] = jnp.zeros((half, half), BF16)
        return carry

    lax.fori_loop(0, z.own, step, 0)


def shared_copy(buffer, slot, send, recv, peer):
    return pltpu.make_async_remote_copy(
        src_ref=buffer.at[slot],
        dst_ref=buffer.at[slot],
        send_sem=send,
        recv_sem=recv,
        device_id=(lax.axis_index("dp"), peer),
        device_id_type=MESH,
    )


class Exchange:
    def __init__(self, z, buffer, send, recv):
        self.z, self.buffer, self.send, self.recv = z, buffer, send, recv

    def copies(self, part):
        me = lax.axis_index("tensor")
        return [
            shared_copy(
                self.buffer.at[part],
                me,
                self.send.at[part, step - 1],
                self.recv.at[part, step - 1],
                (me + step) % self.z.tensor,
            )
            for step in range(1, self.z.tensor)
        ]

    def start(self, part):
        for copy in self.copies(part):
            copy.start()

    def wait(self, part):
        for copy in self.copies(part):
            copy.wait()

    def total(self, part, where):
        terms = [self.buffer[(part, peer) + where].astype(F32) for peer in range(self.z.tensor)]
        return functools.reduce(jnp.add, terms)


def forward_kernel(
    z,
    ids_ref,
    group_ref,
    x_ref,
    cotangent_ref,
    filters_ref,
    gain_one_ref,
    gain_two_ref,
    mixer_hbm,
    ar_hbm,
    gate_hbm,
    up_hbm,
    down_hbm,
    hidden_ref,
    mixed_ref,
    grad_hidden_ref,
    mlp_ref,
    weight_grads_ref,
    gain_ref,
    turned_ref,
    mixer_ref,
    ar_ref,
    gate_ref,
    up_ref,
    down_ref,
    signed_ref,
    lagged_ref,
    turned_mine,
    rows_ref,
    toeplitz_ref,
    conv_ref,
    sum_ref,
    ar_sum_ref,
    normed_two_ref,
    low_ref,
    active_ref,
    gate_pre_ref,
    up_pre_ref,
    part_one,
    part_two,
    load_sem,
    one_send,
    one_recv,
    two_send,
    two_recv,
    turn_send,
    turn_recv,
    turn_own,
):
    line, side, core, across = place(z)
    me = lax.axis_index("dp")
    length, width, rows, half = z.length, z.width, z.rows, z.half

    loads = [
        pltpu.make_async_copy(source, target, load_sem.at[index])
        for index, (source, target) in enumerate(
            (
                (mixer_hbm, mixer_ref),
                (ar_hbm, ar_ref),
                (gate_hbm, gate_ref),
                (up_hbm, up_ref),
                (down_hbm, down_ref),
            )
        )
    ]
    for load in loads:
        load.start()

    barrier = pltpu.get_barrier_semaphore()
    for step in range(1, z.tensor):
        pl.semaphore_signal(barrier, inc=1, device_id=(me, (across + step) % z.tensor), device_id_type=MESH)
    for step in range(1, z.dp):
        pl.semaphore_signal(barrier, inc=1, device_id=((me + step) % z.dp, across), device_id_type=MESH)

    sign = row_sign(length)
    row = lax.broadcasted_iota(jnp.int32, (length, 1), 0)
    for seq in range(z.seqs):
        own_rows = slice(seq * length, (seq + 1) * length)
        values = x_ref[own_rows, :].astype(F32)
        normed = (values * rms_scale(values) * gain_one_ref[...]).astype(BF16)
        signed_ref[0, :, seq * width : (seq + 1) * width] = normed
        normed = normed.astype(F32)
        signed_ref[1, :, seq * width : (seq + 1) * width] = (normed * sign).astype(BF16)
        for lag in range(ORDER):
            shifted = jnp.where(row >= lag, pltpu.roll(normed, lag, 0), 0.0) if lag else normed
            lagged_ref[own_rows, lag * width : (lag + 1) * width] = shifted.astype(BF16)

    turned = signed_ref[0, :, aligned(across % 2, width)].astype(F32).T.astype(BF16)
    turned_mine[...] = turned.reshape(z.dp, z.slice, length)
    rows_ref[...] = filter_rows(filters_ref, True)
    toeplitz_own(z, across * z.own, rows_ref, toeplitz_ref)

    pl.semaphore_wait(barrier, z.dp - 1 + z.tensor - 1)

    def turn_copy(step):
        peer = (me + step) % z.dp
        peer_side = (peer // 2) % 2
        slot = (side + peer_side) % 2 * (2 * z.line) + line * 2 + core
        return pltpu.make_async_remote_copy(
            src_ref=turned_mine.at[peer],
            dst_ref=turned_ref.at[slot],
            send_sem=turn_send.at[step - 1],
            recv_sem=turn_recv.at[step - 1],
            device_id=(peer, across),
            device_id_type=MESH,
        )

    for step in range(1, z.dp):
        turn_copy(step).start()
    turn_mine = pltpu.make_async_copy(turned_mine.at[me], turned_ref.at[line * 2 + core], turn_own)
    turn_mine.start()

    for j in range(2):

        def convolve(k, carry):
            result = dot(toeplitz_ref[k], signed_ref[j]).astype(BF16)
            for seq in range(z.seqs):
                conv_ref[seq * length : (seq + 1) * length, aligned(j * z.own + k, width)] = result[
                    :, seq * width : (seq + 1) * width
                ]
            return carry

        lax.fori_loop(0, z.own, convolve, 0)

    loads[0].wait()
    exchange_one = Exchange(z, part_one, one_send, one_recv)
    depth = z.group * width
    steps = z.own // z.group
    for part in range(2):
        cols = slice(part * half, (part + 1) * half)
        for j in range(2):
            sum_ref[j] = jnp.zeros((rows, half), F32)

            def project(i, carry):
                block = aligned(j * steps + i, depth)
                sum_ref[j] += dot(conv_ref[:, block], mixer_ref[block, cols])
                return carry

            lax.fori_loop(0, steps, project, 0)
        for seq in range(z.seqs):
            own_rows = slice(seq * length, (seq + 1) * length)
            part_one[part, across, own_rows, :] = (sum_ref[0, own_rows, :] + sign * sum_ref[1, own_rows, :]).astype(BF16)
        exchange_one.start(part)

    loads[1].wait()
    ar_sum_ref[...] = dot(lagged_ref[...], ar_ref[...])
    scales = []
    for seq in range(z.seqs):
        scale = jnp.int32(0)
        for group in range(group_ref.shape[0]):
            scale = scale + jnp.where(ids_ref[seq] == group, group_ref[group], 0)
        scales.append(scale.astype(F32))
        own_rows = slice(seq * length, (seq + 1) * length)
        low_ref[own_rows, :] = (cotangent_ref[own_rows, :].astype(F32) * scales[seq]).astype(BF16)

    exchange_one.wait(0)
    exchange_one.wait(1)
    for start in range(0, rows, 128):
        block = slice(start, start + 128)
        summed = jnp.concatenate([exchange_one.total(part, (block, slice(None))) for part in range(2)], axis=1)
        hidden = x_ref[block, :].astype(F32) + (summed + ar_sum_ref[block, :])
        hidden_ref[block, :] = hidden
        normed_two_ref[block, :] = (hidden * rms_scale(hidden) * gain_two_ref[...]).astype(BF16)

    for load in loads[2:]:
        load.wait()
    chunk = min(256, z.hidden)

    def feed(c, carry):
        units = aligned(c, chunk)
        for start in range(0, rows, 256):
            block = slice(start, start + 256)
            gate = dot(normed_two_ref[block, :], gate_ref[:, units])
            up = dot(normed_two_ref[block, :], up_ref[:, units])
            cdf = 0.5 * (1.0 + lax.erf(gate * ROOT_HALF))
            activated = gate * cdf
            active_ref[block, units] = (activated * up).astype(BF16)
            grad = dot_cols(low_ref[block, :], down_ref[units, :])
            density = jnp.exp(-0.5 * gate * gate) * INV_ROOT_TWO_PI
            gate_pre_ref[block, units] = (grad * up * (cdf + gate * density)).astype(BF16)
            up_pre_ref[block, units] = (grad * activated).astype(BF16)
        return carry

    lax.fori_loop(0, z.hidden // chunk, feed, 0)

    exchange_two = Exchange(z, part_two, two_send, two_recv)
    for part in range(2):
        cols = slice(part * half, (part + 1) * half)
        grad = dot_cols(gate_pre_ref[...], gate_ref[cols, :]) + dot_cols(up_pre_ref[...], up_ref[cols, :])
        part_two[part, across] = grad.astype(BF16)
        exchange_two.start(part)

    mlp = dot(active_ref[...], down_ref[...]).astype(BF16)
    mlp_ref[0] = mlp[:, :half]
    mlp_ref[1] = mlp[:, half:]
    for index, (left, right) in enumerate(
        ((normed_two_ref, gate_pre_ref), (normed_two_ref, up_pre_ref), (low_ref, active_ref))
    ):
        weight_grads_ref[index] = (
            dot_rows(left[...], right[...]).astype(BF16).reshape(z.line, 2, 2, z.slice, z.hidden)
        )

    exchange_two.wait(0)
    exchange_two.wait(1)
    gain = jnp.zeros((1, width), F32)
    for start in range(0, rows, 128):
        block = slice(start, start + 128)
        grad = jnp.concatenate([exchange_two.total(part, (block, slice(None))) for part in range(2)], axis=1)
        hidden = hidden_ref[block, :]
        scale = rms_scale(hidden)
        normed = hidden * scale
        gain = gain + jnp.sum(grad * normed, axis=0, keepdims=True)
        weighted = grad * gain_two_ref[...]
        upstream = cotangent_ref[block, :].astype(F32) * scales[start // length]
        grad_hidden = upstream + scale * (weighted - normed * jnp.mean(weighted * normed, axis=-1, keepdims=True))
        grad_hidden_ref[block, :] = grad_hidden
        mixed_ref[block, :] = grad_hidden.astype(BF16)
    gain_ref[...] = jnp.broadcast_to(gain, gain_ref.shape)

    for step in range(1, z.dp):
        turn_copy(step).wait()
    turn_mine.wait()


def backward_kernel(
    z,
    x_ref,
    mixed_ref,
    grad_hidden_ref,
    hidden_ref,
    gain_ref,
    turned_ref,
    filters_ref,
    gain_one_ref,
    ar_ref,
    mlp_hbm,
    mixer_hbm,
    grads_hbm,
    output_ref,
    input_grad_ref,
    mixer_grad_ref,
    ar_grad_ref,
    weight_out_ref,
    gain_out_ref,
    mixer_ref,
    rows_ref,
    plain_rows_ref,
    toeplitz_ref,
    mixed_turned,
    mixed_lagged,
    grad_conv_ref,
    back_ref,
    signed_turned,
    conv_ref,
    sum_ref,
    gathered,
    part_three,
    part_out,
    pair_send,
    pair_recv,
    ring_core,
    ring_own,
    ring_side,
    ring_line,
    gains,
    load_sem,
    out_load_sem,
    own_load_sem,
    gather_send,
    gather_side_send,
    gather_recv,
    three_send,
    three_recv,
    out_send,
    out_recv,
    pair_send_sem,
    pair_recv_sem,
    core_sem,
    side_sem,
    line_send,
    line_recv,
    gain_send,
    gain_recv,
):
    line, side, core, across = place(z)
    me = lax.axis_index("dp")
    length, width, rows, half = z.length, z.width, z.rows, z.half
    lines = z.line
    partner = across + 1 - 2 * (across % 2)
    other = dp_of(line, side, 1 - core)
    opposite = dp_of(line, 1 - side, core)

    depth = z.group * width
    groups = z.own // z.group

    def mixer_load(i):
        return pltpu.make_async_copy(mixer_hbm.at[pl.ds(i * depth, depth), :], mixer_ref.at[i % 2], load_sem.at[i % 2])

    mixer_load(0).start()
    own_load = pltpu.make_async_copy(grads_hbm.at[:, :, :, core], ring_own, own_load_sem)
    own_load.start()
    out_load = pltpu.make_async_copy(mlp_hbm, part_out.at[:, across], out_load_sem)
    out_load.start()

    barrier = pltpu.get_barrier_semaphore()
    for step in range(1, z.tensor):
        pl.semaphore_signal(barrier, inc=1, device_id=(me, (across + step) % z.tensor), device_id_type=MESH)
    for step in range(1, z.dp):
        pl.semaphore_signal(barrier, inc=1, device_id=((me + step) % z.dp, across), device_id_type=MESH)

    def slot_of(far, at):
        return far * (2 * lines) + at * 2 + core

    def block(part, slot):
        return gathered.at[part, aligned(slot, length), :]

    mine = mixed_ref[aligned(across % 2, length), :]
    for part in range(2):
        gathered[part, aligned(slot_of(0, line), length), :] = mine[:, part * half : (part + 1) * half]

    pl.semaphore_wait(barrier, z.dp - 1 + z.tensor - 1)

    def gather_copy(part, source, target, send, peer):
        return pltpu.make_async_remote_copy(
            src_ref=block(part, source),
            dst_ref=block(part, target),
            send_sem=send,
            recv_sem=gather_recv.at[part, target],
            device_id=(peer, across),
            device_id_type=MESH,
        )

    def line_block(part, away, up):
        at = line - away if up else line + away
        slot = slot_of(0, at)
        sems = gather_send.at[part, away, up]
        onward = dp_of(jnp.clip(line + (1 if up else -1), 0, lines - 1), side, core)
        return (
            jnp.logical_and(at >= 0, at < lines),
            lambda: gather_copy(part, slot, slot_of(1, at), sems.at[0], opposite),
            lambda: gather_copy(part, slot, slot, sems.at[1], other),
            lambda: gather_copy(part, slot, slot, sems.at[2], onward),
        )

    def has_onward(up):
        return line + 1 < lines if up else line >= 1

    def gather_round(part, away, act):
        if away == 0:
            _, to_side, to_core, to_line = line_block(part, 0, 1)
            _, _, _, down_line = line_block(part, 0, 0)
            act(to_side())
            pl.when(has_onward(1))(lambda: act(to_line()))
            pl.when(has_onward(0))(lambda: act(down_line()))
            act(to_core())
            return
        for up in (1, 0):
            there, to_side, to_core, to_line = line_block(part, away, up)

            def pass_on(to_side=to_side, to_core=to_core, to_line=to_line, up=up):
                if act is start:
                    to_core().wait_recv()
                act(to_side())
                pl.when(has_onward(up))(lambda: act(to_line()))
                act(to_core())

            pl.when(there)(pass_on)

    def side_round(part, away, act):
        for up in (1, 0) if away else (1,):
            at = line - away if up else line + away

            def pass_on(at=at, up=up):
                slot = slot_of(1, at)
                copy = gather_copy(part, slot, slot, gather_side_send.at[part, away, up], other)
                if act is start:
                    copy.wait_recv()
                act(copy)

            pl.when(jnp.logical_and(at >= 0, at < lines))(pass_on)

    def start(copy):
        copy.start()

    def finish(copy):
        copy.wait_send()

    def await_core(part, far):
        for at in range(lines):
            slot = far * (2 * lines) + at * 2 + 1 - core
            gather_copy(part, slot, slot, gather_side_send.at[part, 0, 0], other).wait_recv()

    gather_round(0, 0, start)

    core_copy = pltpu.make_async_remote_copy(
        src_ref=grads_hbm.at[:, :, :, 1 - core],
        dst_ref=ring_core,
        send_sem=core_sem.at[0],
        recv_sem=core_sem.at[1],
        device_id=(other, across),
        device_id_type=MESH,
    )
    core_copy.start()
    out_load.wait()
    exchange_out = Exchange(z, part_out, out_send, out_recv)
    for part in range(2):
        exchange_out.start(part)

    lane = lax.broadcasted_iota(jnp.int32, (1, length), 1)
    sign = lane_sign(length)
    for seq in range(z.seqs):
        cols = slice(seq * length, (seq + 1) * length)
        turned = mixed_ref[cols, :].astype(F32).T
        mixed_turned[0, :, cols] = turned.astype(BF16)
        mixed_turned[1, :, cols] = (turned * sign).astype(BF16)
        for lag in range(ORDER):
            shifted = jnp.where(lane < length - lag, pltpu.roll(turned, length - lag, 1), 0.0) if lag else turned
            mixed_lagged[lag, :, cols] = shifted.astype(BF16)
    rows_ref[...] = filter_rows(filters_ref, True)
    plain_rows_ref[...] = filter_rows(filters_ref, False)
    toeplitz_own(z, across * z.own, rows_ref, toeplitz_ref)

    gather_round(0, 1, start)
    gather_round(1, 0, start)

    for j in range(2):
        back_ref[j] = jnp.zeros(back_ref.shape[1:], F32)
        for g in range(groups):
            i = j * groups + g
            if i + 1 < 2 * groups:
                mixer_load(i + 1).start()
            mixer_load(i).wait()

            def project(k, carry):
                result = dot(mixer_ref[i % 2, aligned(k, width), :], mixed_turned[j]).astype(BF16)
                for seq in range(z.seqs):
                    grad_conv_ref[seq * width : (seq + 1) * width, aligned(k, length)] = result[
                        :, seq * length : (seq + 1) * length
                    ]
                return carry

            lax.fori_loop(0, z.group, project, 0)
            taps = toeplitz_ref[g * z.group : (g + 1) * z.group].reshape(z.group * length, length)
            back_ref[j] += dot(grad_conv_ref[...], taps)
    exchange_three = Exchange(z, part_three, three_send, three_recv)
    for seq in range(z.seqs):
        cols = slice(seq * width, (seq + 1) * width)
        part_three[seq, across] = (back_ref[0, cols, :] + sign * back_ref[1, cols, :]).astype(BF16)
        exchange_three.start(seq)

    for away in range(2, lines):
        gather_round(0, away, start)
    for away in range(lines):
        side_round(0, away, start)

    own_load.wait()
    core_copy.wait()
    side_copy = pltpu.make_async_remote_copy(
        src_ref=ring_own.at[:, :, 1 - side],
        dst_ref=ring_side,
        send_sem=side_sem.at[0],
        recv_sem=side_sem.at[1],
        device_id=(opposite, across),
        device_id_type=MESH,
    )
    for index in range(3):
        for at in range(lines):
            for where in range(2):
                ring_own[index, at, where] = (
                    ring_own[index, at, where].astype(F32) + ring_core[index, at, where].astype(F32)
                ).astype(BF16)
    side_copy.start()

    for away in range(1, lines):
        gather_round(1, away, start)

    slots = z.dp
    for slot in range(slots):
        signed_turned[0, slot * z.slice : (slot + 1) * z.slice, :] = turned_ref[slot]
        signed_turned[1, slot * z.slice : (slot + 1) * z.slice, :] = (turned_ref[slot].astype(F32) * sign).astype(BF16)
    half_length = length // 2
    tap_row = lax.broadcasted_iota(jnp.int32, (half_length, length), 0)
    tap_lane = lax.broadcasted_iota(jnp.int32, (half_length, length), 1)
    pair_rows = 2 * z.own * z.slice

    def convolve(k, carry):
        values = jnp.broadcast_to(
            plain_rows_ref[pl.ds((across - across % 2) * z.own + k, 1), :], (half_length, length)
        )
        upper = jnp.where(tap_lane >= tap_row, pltpu.roll(values, 0, 1, stride=1, stride_axis=0), 0.0)
        lower = jnp.concatenate([jnp.zeros((half_length, half_length), F32), upper[:, :half_length]], axis=1)
        taps = jnp.concatenate([upper, lower], axis=0).astype(BF16)
        first = (k // z.own) * pair_rows + (k % z.own) * z.slice
        for j in range(2):
            result = dot(signed_turned[j], taps)
            if j:
                result = result * sign
            result = result.astype(BF16)
            at = pl.ds(pl.multiple_of(first + j * z.own * z.slice, z.slice), z.slice)
            for slot in range(slots):
                conv_ref[at, slot * length : (slot + 1) * length] = result[slot * z.slice : (slot + 1) * z.slice, :]
        return carry

    lax.fori_loop(0, 2 * z.own, convolve, 0)
    for slot in range(slots):
        normed = turned_ref[slot].astype(F32)
        for lag in range(ORDER):
            shifted = jnp.where(lane >= lag, pltpu.roll(normed, lag, 1), 0.0) if lag else normed
            at = 2 * pair_rows + lag * z.slice
            conv_ref[at : at + z.slice, slot * length : (slot + 1) * length] = shifted.astype(BF16)

    for away in range(lines):
        side_round(1, away, start)

    back_ref[0, :width, :] = jnp.zeros((width, length), F32)
    ar_back = [
        functools.reduce(
            jnp.add,
            [
                dot(ar_ref[lag * width : (lag + 1) * width, :], mixed_lagged[lag, :, seq * length : (seq + 1) * length])
                for lag in range(ORDER)
            ],
        )
        for seq in range(z.seqs)
    ]
    for seq in range(z.seqs):
        back_ref[0, seq * width : (seq + 1) * width, :] = ar_back[seq]
    gain_sum = jnp.zeros((1, width), F32)
    for seq in range(z.seqs):
        exchange_three.wait(seq)
        grad_turned = exchange_three.total(seq, ()) + back_ref[0, seq * width : (seq + 1) * width, :]
        grad = grad_turned.T
        own_rows = slice(seq * length, (seq + 1) * length)
        values = x_ref[own_rows, :].astype(F32)
        scale = rms_scale(values)
        normed = values * scale
        gain_sum = gain_sum + jnp.sum(grad * normed, axis=0, keepdims=True)
        weighted = grad * gain_one_ref[...]
        input_grad_ref[own_rows, :] = grad_hidden_ref[own_rows, :] + scale * (
            weighted - normed * jnp.mean(weighted * normed, axis=-1, keepdims=True)
        )
    gains[me] = jnp.concatenate(
        [gain_ref[0:1, :], gain_sum, jnp.zeros((6, width), F32)], axis=0
    )

    def gain_copy(step):
        return pltpu.make_async_remote_copy(
            src_ref=gains.at[me],
            dst_ref=gains.at[me],
            send_sem=gain_send.at[step - 1],
            recv_sem=gain_recv.at[step - 1],
            device_id=((me + step) % z.dp, across),
            device_id_type=MESH,
        )

    for step in range(1, z.dp):
        gain_copy(step).start()

    side_copy.wait()
    for index in range(3):
        for at in range(lines):
            ring_side[index, at] = (
                ring_side[index, at].astype(F32) + ring_own[index, at, side].astype(F32)
            ).astype(BF16)

    def line_copy(step):
        target = (line + step) % lines
        return pltpu.make_async_remote_copy(
            src_ref=ring_side.at[:, target],
            dst_ref=ring_line.at[step - 1],
            send_sem=line_send.at[step - 1],
            recv_sem=line_recv.at[step - 1],
            device_id=(dp_of(target, side, core), across),
            device_id_type=MESH,
        )

    for step in range(1, lines):
        line_copy(step).start()

    pair_copies = []
    near = slots // 2 * length
    for part in range(2):
        cols = slice(part * half, (part + 1) * half)
        for far in range(2):
            await_core(part, far)
            tokens = slice(far * near, (far + 1) * near)
            for first in range(0, 2 * pair_rows, pair_rows):
                taken = slice(first, first + pair_rows)
                product = dot(conv_ref[taken, tokens], gathered[part, tokens, :])
                sum_ref[taken, cols] = product if far == 0 else sum_ref[taken, cols] + product
            taken = slice(2 * pair_rows, 2 * pair_rows + ORDER * z.slice)
            product = dot(conv_ref[taken, tokens], gathered[part, tokens, :])
            sum_ref[taken, cols] = product if far == 0 else sum_ref[taken, cols] + product
        pair_send[part, :pair_rows, :] = sum_ref[aligned(1 - across % 2, pair_rows), cols].astype(BF16)
        pair_send[part, pair_rows:, :] = sum_ref[2 * pair_rows :, cols].astype(BF16)
        copy = pltpu.make_async_remote_copy(
            src_ref=pair_send.at[part],
            dst_ref=pair_recv.at[part],
            send_sem=pair_send_sem.at[part],
            recv_sem=pair_recv_sem.at[part],
            device_id=(me, partner),
            device_id_type=MESH,
        )
        copy.start()
        pair_copies.append(copy)

    for part in range(2):
        exchange_out.wait(part)
        cols = slice(part * half, (part + 1) * half)
        output_ref[:, cols] = hidden_ref[:, cols] + exchange_out.total(part, ())

    for step in range(1, lines):
        line_copy(step).wait()
    for index in range(3):
        total = ring_side[index, line].astype(F32)
        for step in range(1, lines):
            total = total + ring_line[step - 1, index].astype(F32)
        weight_out_ref[index] = total

    for step in range(1, z.dp):
        gain_copy(step).wait()
    gain_out_ref[...] = functools.reduce(jnp.add, [gains[index] for index in range(z.dp)])

    for part in range(2):
        cols = slice(part * half, (part + 1) * half)
        pair_copies[part].wait()
        mixer_grad_ref[:, cols] = sum_ref[aligned(across % 2, pair_rows), cols] + pair_recv[
            part, :pair_rows, :
        ].astype(F32)
        ar_grad_ref[:, cols] = pair_send[part, pair_rows:, :].astype(F32) + pair_recv[part, pair_rows:, :].astype(F32)

    for part in range(2):
        for away in range(lines):
            gather_round(part, away, finish)
            side_round(part, away, finish)


VMEM_SPEC = pl.BlockSpec(memory_space=pltpu.VMEM)
HBM_SPEC = pl.BlockSpec(memory_space=pl.ANY)
SMEM_SPEC = pl.BlockSpec(memory_space=pltpu.SMEM)
DMA = pltpu.SemaphoreType.DMA


def shape(dims, dtype):
    return jax.ShapeDtypeStruct(dims, dtype)


def body(
    mesh_shape,
    inputs,
    cotangent,
    group_ids,
    group_weights,
    filters,
    gain_mixer,
    mixer_weights,
    ar_weights,
    gain_mlp,
    w_gate,
    w_up,
    w_down,
):
    z = Sizes(mesh_shape, inputs.shape, mixer_weights.shape, filters.shape, w_gate.shape)
    length, width, rows, half = z.length, z.width, z.rows, z.half
    x = inputs.reshape(rows, width)
    mixer = mixer_weights.reshape(2 * z.own * width, width)
    ar = ar_weights.reshape(ORDER * width, width)
    gain_one = gain_mixer.reshape(1, width)
    others = z.tensor - 1
    exchange = [DMA((2, others)), DMA((2, others))]
    hidden, mixed, grad_hidden, mlp, weight_grads, gain, turned = pl.pallas_call(
        functools.partial(forward_kernel, z),
        name="forward",
        out_shape=(
            shape((rows, width), F32),
            shape((rows, width), BF16),
            shape((rows, width), F32),
            shape((2, rows, half), BF16),
            shape((3, z.line, 2, 2, z.slice, z.hidden), BF16),
            shape((8, width), F32),
            shape((z.dp, z.slice, length), BF16),
        ),
        in_specs=[SMEM_SPEC] * 2 + [VMEM_SPEC] * 5 + [HBM_SPEC] * 5,
        out_specs=(VMEM_SPEC,) * 7,
        scratch_shapes=[
            pltpu.VMEM(mixer.shape, BF16),
            pltpu.VMEM(ar.shape, BF16),
            pltpu.VMEM(w_gate.shape, BF16),
            pltpu.VMEM(w_up.shape, BF16),
            pltpu.VMEM(w_down.shape, BF16),
            pltpu.VMEM((2, length, z.seqs * width), BF16),
            pltpu.VMEM((rows, ORDER * width), BF16),
            pltpu.VMEM((z.dp, z.slice, length), BF16),
            pltpu.VMEM((z.filters, length), F32),
            pltpu.VMEM((z.own, length, length), BF16),
            pltpu.VMEM((rows, 2 * z.own * width), BF16),
            pltpu.VMEM((2, rows, half), F32),
            pltpu.VMEM((rows, width), F32),
            pltpu.VMEM((rows, width), BF16),
            pltpu.VMEM((rows, width), BF16),
            pltpu.VMEM((rows, z.hidden), BF16),
            pltpu.VMEM((rows, z.hidden), BF16),
            pltpu.VMEM((rows, z.hidden), BF16),
            pltpu.VMEM((2, z.tensor, rows, half), BF16),
            pltpu.VMEM((2, z.tensor, rows, half), BF16),
            DMA((5,)),
            *exchange,
            *exchange,
            DMA((z.dp - 1,)),
            DMA((z.dp - 1,)),
            DMA,
        ],
        compiler_params=pltpu.CompilerParams(
            collective_id=1, has_side_effects=True, vmem_limit_bytes=60 * MIB
        ),
    )(
        group_ids,
        group_weights,
        x,
        cotangent.reshape(rows, width),
        filters,
        gain_one,
        gain_mlp.reshape(1, width),
        mixer,
        ar,
        w_gate,
        w_up,
        w_down,
    )
    pair_rows = 2 * z.own * z.slice
    ar_rows = ORDER * z.slice
    output, input_grad, mixer_grad, ar_grad, weight_out, gains = pl.pallas_call(
        functools.partial(backward_kernel, z),
        name="backward",
        out_shape=(
            shape((rows, width), F32),
            shape((rows, width), F32),
            shape((pair_rows, width), F32),
            shape((ar_rows, width), F32),
            shape((3, z.slice, z.hidden), F32),
            shape((8, width), F32),
        ),
        in_specs=[VMEM_SPEC] * 9 + [HBM_SPEC] * 3,
        out_specs=(VMEM_SPEC,) * 6,
        scratch_shapes=[
            pltpu.VMEM((2, z.group * width, width), BF16),
            pltpu.VMEM((z.filters, length), F32),
            pltpu.VMEM((z.filters, length), F32),
            pltpu.VMEM((z.own, length, length), BF16),
            pltpu.VMEM((2, width, rows), BF16),
            pltpu.VMEM((ORDER, width, rows), BF16),
            pltpu.VMEM((z.seqs * width, z.group * length), BF16),
            pltpu.VMEM((2, z.seqs * width, length), F32),
            pltpu.VMEM((2, z.dp * z.slice, length), BF16),
            pltpu.VMEM((2 * pair_rows + ar_rows, z.dp * length), BF16),
            pltpu.VMEM((2 * pair_rows + ar_rows, width), F32),
            pltpu.VMEM((2, z.dp * length, half), BF16),
            pltpu.VMEM((z.seqs, z.tensor, width, length), BF16),
            pltpu.VMEM((2, z.tensor, rows, half), BF16),
            pltpu.VMEM((2, pair_rows + ar_rows, half), BF16),
            pltpu.VMEM((2, pair_rows + ar_rows, half), BF16),
            pltpu.VMEM((3, z.line, 2, z.slice, z.hidden), BF16),
            pltpu.VMEM((3, z.line, 2, z.slice, z.hidden), BF16),
            pltpu.VMEM((3, z.line, z.slice, z.hidden), BF16),
            pltpu.VMEM((max(1, z.line - 1), 3, z.slice, z.hidden), BF16),
            pltpu.VMEM((z.dp, 8, width), F32),
            DMA((2,)),
            DMA,
            DMA,
            DMA((2, z.line, 2, 3)),
            DMA((2, z.line, 2)),
            DMA((2, z.dp)),
            *[DMA((z.seqs, others)), DMA((z.seqs, others))],
            *exchange,
            DMA((2,)),
            DMA((2,)),
            DMA((2,)),
            DMA((2,)),
            DMA((max(1, z.line - 1),)),
            DMA((max(1, z.line - 1),)),
            DMA((z.dp - 1,)),
            DMA((z.dp - 1,)),
        ],
        compiler_params=pltpu.CompilerParams(
            collective_id=2, has_side_effects=True, vmem_limit_bytes=62 * MIB
        ),
    )(
        x,
        mixed,
        grad_hidden,
        hidden,
        gain,
        turned,
        filters,
        gain_one,
        ar,
        mlp,
        mixer,
        weight_grads,
    )
    first = lax.axis_index("dp") * z.slice
    gain_slices = lax.dynamic_slice_in_dim(gains, first, z.slice, 1)
    return (
        output.reshape(inputs.shape),
        input_grad.reshape(inputs.shape),
        gain_slices[1],
        mixer_grad.reshape(2, z.own, z.slice, width),
        ar_grad.reshape(ORDER, z.slice, width),
        gain_slices[0],
        weight_out[0],
        weight_out[1],
        weight_out[2].T,
    )


def solution(mesh):
    placed = (
        P("dp", None, None),
        P("dp", None, None),
        P("dp"),
        P(),
        P(),
        P(),
        P(None, "tensor", None, None),
        P(),
        P(),
        P(None, "tensor"),
        P(None, "tensor"),
        P("tensor", None),
    )
    return jax.shard_map(
        functools.partial(body, dict(mesh.shape)),
        mesh=mesh,
        in_specs=placed,
        out_specs=(
            P("dp", None, None),
            P("dp", None, None),
            P("dp"),
            P(None, "tensor", "dp", None),
            P(None, "dp", None),
            P("dp"),
            P("dp", "tensor"),
            P("dp", "tensor"),
            P("tensor", "dp"),
        ),
        check_vma=False,
    )
```

```python
import functools

import jax
import jax.numpy as jnp
from jax import lax
from jax.experimental import pallas as pl
from jax.experimental.pallas import tpu as pltpu
from jax.sharding import PartitionSpec as P

F32 = jnp.float32
BF16 = jnp.bfloat16
MESH = pl.DeviceIdType.MESH
EPSILON = 1e-06
ROOT_HALF = 0.7071067811865476
INV_ROOT_TWO_PI = 0.3989422804014327
ORDER = 3
MIB = 2**20


def dot(left, right):
    return jnp.dot(left, right, preferred_element_type=F32)


def dot_cols(left, right):
    return lax.dot_general(left, right, (((1,), (1,)), ((), ())), preferred_element_type=F32)


def dot_rows(left, right):
    return lax.dot_general(left, right, (((0,), (0,)), ((), ())), preferred_element_type=F32)


def rms_scale(values):
    return lax.rsqrt(jnp.mean(values * values, axis=-1, keepdims=True) + EPSILON)


def row_sign(rows):
    odd = lax.broadcasted_iota(jnp.int32, (rows, 1), 0) % 2
    return 1.0 - 2.0 * odd.astype(F32)


def lane_sign(lanes):
    odd = lax.broadcasted_iota(jnp.int32, (1, lanes), 1) % 2
    return 1.0 - 2.0 * odd.astype(F32)


def aligned(index, step):
    return pl.ds(pl.multiple_of(index * step, step), step)


class Sizes:
    def __init__(self, mesh_shape, inputs, mixer_weights, filters, w_gate):
        self.seqs, self.length, self.width = inputs
        self.rows = self.seqs * self.length
        self.dp = mesh_shape["dp"]
        self.tensor = mesh_shape["tensor"]
        self.line = self.dp // 4
        self.own = mixer_weights[1]
        self.filters = filters[0]
        self.hidden = w_gate[1]
        self.slice = self.width // self.dp
        self.group = max(g for g in range(1, 5) if self.own % g == 0)
        self.depth = self.group * self.width
        self.chunks = 2 * self.own // self.group
        self.half = self.width // 2
        self.near = self.dp // 2 * self.length
        self.pair_rows = 2 * self.own * self.slice
        self.ar_rows = ORDER * self.slice
        self.all_rows = 2 * self.pair_rows + self.ar_rows


def place(z):
    dp = lax.axis_index("dp")
    return dp // 4, (dp // 2) % 2, dp % 2, lax.axis_index("tensor")


def dp_of(line, side, core):
    return (line * 2 + side) * 2 + core


def reversed_rows(filters_ref):
    length = filters_ref.shape[1]
    source = lax.broadcasted_iota(jnp.int32, (length, length), 0)
    target = lax.broadcasted_iota(jnp.int32, (length, length), 1)
    pick = (source == (length + length // 2 - target) % length).astype(BF16)
    return dot(filters_ref[...], pick)


def toeplitz_own(z, own_first, rows_ref, out_ref):
    length, half = z.length, z.length // 2
    lane = lax.broadcasted_iota(jnp.int32, (half, length), 1)
    row = lax.broadcasted_iota(jnp.int32, (half, length), 0)

    def step(k, carry):
        values = jnp.broadcast_to(rows_ref[pl.ds(own_first + k, 1), :], (half, length))
        rolled = pltpu.roll(values, 0, 1, stride=1, stride_axis=0)
        lower = jnp.where(lane <= row + half, rolled, 0.0).astype(BF16)
        out_ref[k, half:, :] = lower
        out_ref[k, :half, :half] = lower[:, half:]
        out_ref[k, :half, half:] = jnp.zeros((half, half), BF16)
        return carry

    lax.fori_loop(0, z.own, step, 0)


def shared_copy(buffer, slot, send, recv, peer):
    return pltpu.make_async_remote_copy(
        src_ref=buffer.at[slot],
        dst_ref=buffer.at[slot],
        send_sem=send,
        recv_sem=recv,
        device_id=(lax.axis_index("dp"), peer),
        device_id_type=MESH,
    )


class Exchange:
    def __init__(self, z, buffer, send, recv):
        self.z, self.buffer, self.send, self.recv = z, buffer, send, recv

    def copies(self, part):
        me = lax.axis_index("tensor")
        return [
            shared_copy(
                self.buffer.at[part],
                me,
                self.send.at[part, step - 1],
                self.recv.at[part, step - 1],
                (me + step) % self.z.tensor,
            )
            for step in range(1, self.z.tensor)
        ]

    def start(self, part):
        for copy in self.copies(part):
            copy.start()

    def wait(self, part):
        for copy in self.copies(part):
            copy.wait()

    def total(self, part, where):
        terms = [self.buffer[(part, peer) + where].astype(F32) for peer in range(self.z.tensor)]
        return functools.reduce(jnp.add, terms)


def block_kernel(
    z,
    ids_ref,
    group_ref,
    x_ref,
    cotangent_ref,
    filters_ref,
    gain_one_ref,
    gain_two_ref,
    mixer_hbm,
    ar_hbm,
    gate_hbm,
    up_hbm,
    down_hbm,
    output_hbm,
    input_grad_hbm,
    mixer_grad_hbm,
    ar_grad_hbm,
    weight_grad_hbm,
    gain_grad_hbm,
    output_ref,
    input_grad_ref,
    ar_grad_ref,
    weight_grad_ref,
    gain_grad_ref,
    mixer_ref,
    ar_ref,
    gate_ref,
    up_ref,
    down_ref,
    signed_ref,
    lagged_ref,
    turned_mine,
    turned_ref,
    signed_turned,
    rows_ref,
    plain_rows_ref,
    toeplitz_ref,
    conv_ref,
    conv_near,
    sum_ref,
    normed_two_ref,
    low_ref,
    active_ref,
    gate_pre_ref,
    up_pre_ref,
    mixed_ref,
    mixed_turned,
    grad_conv_ref,
    back_ref,
    ar_back_ref,
    gathered,
    part_one,
    part_two,
    part_three,
    part_out,
    pair_send,
    pair_recv,
    grads_ref,
    ring_core,
    ring_side,
    ring_line,
    gains,
    mixer_sem,
    load_sem,
    write_sem,
    turn_own,
    turn_send,
    turn_recv,
    one_send,
    one_recv,
    two_send,
    two_recv,
    three_send,
    three_recv,
    out_send,
    out_recv,
    gather_send,
    gather_side_send,
    gather_recv,
    core_send,
    core_recv,
    side_send,
    side_recv,
    line_send,
    line_recv,
    pair_send_sem,
    pair_recv_sem,
    gain_send,
    gain_recv,
):
    line, side, core, across = place(z)
    me = lax.axis_index("dp")
    length, width, rows, half = z.length, z.width, z.rows, z.half
    lines, own, steps = z.line, z.own, z.own // z.group
    other = dp_of(line, side, 1 - core)
    opposite = dp_of(line, 1 - side, core)
    partner = across + 1 - 2 * (across % 2)
    own_seq = (across + core) % 2

    def mixer_load(q):
        slot = q % 2
        source = mixer_hbm.at[aligned(q % z.chunks, z.depth), :]
        return pltpu.make_async_copy(source, mixer_ref.at[slot], mixer_sem.at[slot])

    loads = [
        pltpu.make_async_copy(source, target, load_sem.at[index])
        for index, (source, target) in enumerate(
            ((ar_hbm, ar_ref), (gate_hbm, gate_ref), (up_hbm, up_ref), (down_hbm, down_ref))
        )
    ]
    mixer_load(0).start()
    mixer_load(1).start()
    for load in loads:
        load.start()

    barrier = pltpu.get_barrier_semaphore()
    for step in range(1, z.tensor):
        pl.semaphore_signal(barrier, inc=1, device_id=(me, (across + step) % z.tensor), device_id_type=MESH)
    for step in range(1, z.dp):
        pl.semaphore_signal(barrier, inc=1, device_id=((me + step) % z.dp, across), device_id_type=MESH)

    sign = row_sign(length)
    turned_sign = lane_sign(length)
    for seq in range(z.seqs):
        values = x_ref[seq * length : (seq + 1) * length, :].astype(F32)
        normed = (values * rms_scale(values) * gain_one_ref[...]).astype(BF16)
        signed_ref[seq, :, :width] = normed
        signed_ref[seq, :, width:] = (normed.astype(F32) * sign).astype(BF16)
    rows_ref[...] = reversed_rows(filters_ref)
    plain_rows_ref[...] = filters_ref[...].astype(F32)
    toeplitz_own(z, across * own, rows_ref, toeplitz_ref)

    exchange_one = Exchange(z, part_one, one_send, one_recv)
    exchange_two = Exchange(z, part_two, two_send, two_recv)
    exchange_three = Exchange(z, part_three, three_send, three_recv)
    exchange_out = Exchange(z, part_out, out_send, out_recv)

    def seq_rows(seq):
        return slice(seq * length, (seq + 1) * length)

    def mix(seq):
        def convolve(k, carry):
            result = dot(toeplitz_ref[k], signed_ref[seq]).astype(BF16)
            for j in range(2):
                chunk = j * steps + k // z.group
                conv_near[aligned(chunk, length), aligned(k % z.group, width)] = result[:, j * width : (j + 1) * width]
            return carry

        lax.fori_loop(0, own, convolve, 0)
        sum_ref[: 2 * length, :] = jnp.zeros((2 * length, width), F32)

        def project(i, carry):
            q = seq * z.chunks + i
            mixer_load(q).wait()
            sum_ref[aligned(i // steps, length), :] += dot(conv_near[aligned(i, length), : z.depth], mixer_ref[q % 2])
            mixer_load(q + 2).start()
            return carry

        lax.fori_loop(0, z.chunks, project, 0)
        part_one[seq, across] = (sum_ref[:length, :] + sign * sum_ref[length : 2 * length, :]).astype(BF16)

    mix(0)
    pl.semaphore_wait(barrier, z.dp - 1 + z.tensor - 1)
    exchange_one.start(0)

    turned_mine[...] = signed_ref[own_seq, :, :width].astype(F32).T.astype(BF16).reshape(z.dp, z.slice, length)

    def turn_copy(step):
        peer = (me + step) % z.dp
        far = (side + (peer // 2) % 2) % 2
        return pltpu.make_async_remote_copy(
            src_ref=turned_mine.at[peer],
            dst_ref=turned_ref.at[far * (2 * lines) + line * 2 + core],
            send_sem=turn_send.at[step - 1],
            recv_sem=turn_recv.at[step - 1],
            device_id=(peer, across),
            device_id_type=MESH,
        )

    for step in range(1, z.dp):
        turn_copy(step).start()
    turn_mine = pltpu.make_async_copy(turned_mine.at[me], turned_ref.at[line * 2 + core], turn_own)
    turn_mine.start()

    mix(1)
    exchange_one.start(1)

    row = lax.broadcasted_iota(jnp.int32, (length, 1), 0)
    loads[0].wait()
    scales = []
    for seq in range(z.seqs):
        own_rows = seq_rows(seq)
        normed = signed_ref[seq, :, :width].astype(F32)
        for lag in range(ORDER):
            shifted = jnp.where(row >= lag, pltpu.roll(normed, lag, 0), 0.0) if lag else normed
            lagged_ref[own_rows, lag * width : (lag + 1) * width] = shifted.astype(BF16)
        scale = jnp.int32(0)
        for group in range(group_ref.shape[0]):
            scale = scale + jnp.where(ids_ref[seq] == group, group_ref[group], 0)
        scales.append(scale.astype(F32))
        low_ref[own_rows, :] = (cotangent_ref[own_rows, :].astype(F32) * scales[seq]).astype(BF16)
    output_ref[...] = dot(lagged_ref[...], ar_ref[...])

    chunk = min(256, z.hidden)

    def feed_forward(seq):
        own_rows = seq_rows(seq)
        exchange_one.wait(seq)
        for start in range(seq * length, (seq + 1) * length, 128):
            block = slice(start, start + 128)
            inside = slice(start - seq * length, start - seq * length + 128)
            hidden = x_ref[block, :].astype(F32) + (exchange_one.total(seq, (inside,)) + output_ref[block, :])
            output_ref[block, :] = hidden
            normed_two_ref[block, :] = (hidden * rms_scale(hidden) * gain_two_ref[...]).astype(BF16)
        if seq == 0:
            for load in loads[1:]:
                load.wait()

        def feed(c, carry):
            units = aligned(c, chunk)
            gate = dot(normed_two_ref[own_rows, :], gate_ref[:, units])
            up = dot(normed_two_ref[own_rows, :], up_ref[:, units])
            cdf = 0.5 * (1.0 + lax.erf(gate * ROOT_HALF))
            activated = gate * cdf
            active_ref[own_rows, units] = (activated * up).astype(BF16)
            grad = dot_cols(low_ref[own_rows, :], down_ref[units, :])
            density = jnp.exp(-0.5 * gate * gate) * INV_ROOT_TWO_PI
            gate_pre_ref[own_rows, units] = (grad * up * (cdf + gate * density)).astype(BF16)
            up_pre_ref[own_rows, units] = (grad * activated).astype(BF16)
            return carry

        lax.fori_loop(0, z.hidden // chunk, feed, 0)
        grad = dot_cols(gate_pre_ref[own_rows, :], gate_ref[...]) + dot_cols(up_pre_ref[own_rows, :], up_ref[...])
        part_two[seq, across] = grad.astype(BF16)
        exchange_two.start(seq)

    for seq in range(z.seqs):
        feed_forward(seq)

    def core_copy(index):
        return pltpu.make_async_remote_copy(
            src_ref=grads_ref.at[index, :, :, 1 - core],
            dst_ref=ring_core.at[index],
            send_sem=core_send.at[index],
            recv_sem=core_recv.at[index],
            device_id=(other, across),
            device_id_type=MESH,
        )

    for index, (left, right) in enumerate(
        ((normed_two_ref, gate_pre_ref), (normed_two_ref, up_pre_ref), (low_ref, active_ref))
    ):
        product = dot_rows(left[...], right[...]).astype(BF16)
        grads_ref[index] = product.reshape(lines, 2, 2, z.slice, z.hidden)
        core_copy(index).start()
    for seq in range(z.seqs):
        part_out[seq, across] = dot(active_ref[seq_rows(seq), :], down_ref[...]).astype(BF16)
        exchange_out.start(seq)

    def slot_of(far, at):
        return far * (2 * lines) + at * 2 + core

    def gather_copy(part, source, target, send, peer):
        return pltpu.make_async_remote_copy(
            src_ref=gathered.at[part, aligned(source, length), :],
            dst_ref=gathered.at[part, aligned(target, length), :],
            send_sem=send,
            recv_sem=gather_recv.at[part, target],
            device_id=(peer, across),
            device_id_type=MESH,
        )

    def line_block(part, away, up):
        at = line - away if up else line + away
        slot = slot_of(0, at)
        sems = gather_send.at[part, away, up]
        onward = dp_of(jnp.clip(line + (1 if up else -1), 0, lines - 1), side, core)
        return (
            jnp.logical_and(at >= 0, at < lines),
            lambda: gather_copy(part, slot, slot_of(1, at), sems.at[0], opposite),
            lambda: gather_copy(part, slot, slot, sems.at[1], other),
            lambda: gather_copy(part, slot, slot, sems.at[2], onward),
        )

    def has_onward(up):
        return line + 1 < lines if up else line >= 1

    def start_copy(copy):
        copy.start()

    def finish_copy(copy):
        copy.wait_send()

    def line_round(part, away, act):
        if away == 0:
            _, to_side, to_core, to_line = line_block(part, 0, 1)
            _, _, _, down_line = line_block(part, 0, 0)
            pl.when(has_onward(1))(lambda: act(to_line()))
            pl.when(has_onward(0))(lambda: act(down_line()))
            act(to_side())
            act(to_core())
            return
        for up in (1, 0):
            there, to_side, to_core, to_line = line_block(part, away, up)

            def pass_on(to_side=to_side, to_core=to_core, to_line=to_line, up=up):
                if act is start_copy:
                    to_core().wait_recv()
                pl.when(has_onward(up))(lambda: act(to_line()))
                act(to_side())
                act(to_core())

            pl.when(there)(pass_on)

    def side_round(part, away, act):
        for up in (1, 0) if away else (1,):
            at = line - away if up else line + away

            def pass_on(at=at, up=up):
                slot = slot_of(1, at)
                copy = gather_copy(part, slot, slot, gather_side_send.at[part, away, up], other)
                if act is start_copy:
                    copy.wait_recv()
                act(copy)

            pl.when(jnp.logical_and(at >= 0, at < lines))(pass_on)

    def await_core(part, far):
        for at in range(lines):
            slot = far * (2 * lines) + at * 2 + 1 - core
            gather_copy(part, slot, slot, gather_side_send.at[part, 0, 0], other).wait_recv()

    def mixed_gradient(seq):
        exchange_two.wait(seq)
        gain = jnp.zeros((1, width), F32)
        for start in range(seq * length, (seq + 1) * length, 128):
            block = slice(start, start + 128)
            inside = slice(start - seq * length, start - seq * length + 128)
            grad = exchange_two.total(seq, (inside,))
            hidden = output_ref[block, :]
            scale = rms_scale(hidden)
            normed = hidden * scale
            gain = gain + jnp.sum(grad * normed, axis=0, keepdims=True)
            weighted = grad * gain_two_ref[...]
            upstream = cotangent_ref[block, :].astype(F32) * scales[seq]
            grad_hidden = upstream + scale * (weighted - normed * jnp.mean(weighted * normed, axis=-1, keepdims=True))
            input_grad_ref[block, :] = grad_hidden
            mixed_ref[block, :] = grad_hidden.astype(BF16)

        def send():
            for part in range(2):
                gathered[part, aligned(slot_of(0, line), length), :] = mixed_ref[
                    seq_rows(seq), part * half : (part + 1) * half
                ]
                line_round(part, 0, start_copy)

        pl.when(own_seq == seq)(send)
        return gain

    def events_of(late):
        early = []
        for away in range(lines):
            for part in range(2):
                if away:
                    early.append(functools.partial(line_round, part, away, start_copy))
            if away >= 1:
                for part in range(2):
                    early.append(functools.partial(side_round, part, away - 1, start_copy))
        for part in range(2):
            early.append(functools.partial(side_round, part, lines - 1, start_copy))
        return [lambda event=event: pl.when(own_seq == late)(event) for event in early]

    def side_copy(index):
        return pltpu.make_async_remote_copy(
            src_ref=grads_ref.at[index, :, 1 - side, core],
            dst_ref=ring_side.at[index],
            send_sem=side_send.at[index],
            recv_sem=side_recv.at[index],
            device_id=(opposite, across),
            device_id_type=MESH,
        )

    def reduce_core(index):
        core_copy(index).wait()
        for at in range(lines):
            for where in range(2):
                grads_ref[index, at, where, core] = (
                    grads_ref[index, at, where, core].astype(F32) + ring_core[index, at, where].astype(F32)
                ).astype(BF16)
        side_copy(index).start()

    def line_copy(index, step):
        target = (line + step) % lines
        return pltpu.make_async_remote_copy(
            src_ref=ring_side.at[index, target],
            dst_ref=ring_line.at[index, step - 1],
            send_sem=line_send.at[index, step - 1],
            recv_sem=line_recv.at[index, step - 1],
            device_id=(dp_of(target, side, core), across),
            device_id_type=MESH,
        )

    def reduce_side(index):
        side_copy(index).wait()
        for at in range(lines):
            ring_side[index, at] = (
                ring_side[index, at].astype(F32) + grads_ref[index, at, side, core].astype(F32)
            ).astype(BF16)
        for step in range(1, lines):
            line_copy(index, step).start()

    def write(source, target, index):
        copy = pltpu.make_async_copy(source, target, write_sem.at[index])
        copy.start()
        return copy

    gain_two = mixed_gradient(0)

    positions = 2 * z.chunks + 4
    plan = {at: [] for at in range(positions)}
    for late in range(2):
        events = events_of(late)
        first, last = (2, 2 * z.chunks) if late == 0 else (min(5, z.chunks), positions - 1)
        for index, event in enumerate(events):
            plan[first + index * (last - first) // len(events)].append(event)
    for index in range(3):
        plan[index].append(functools.partial(reduce_core, index))
        plan[z.chunks + 2 + 2 * index if z.chunks > 2 else positions - 1].append(functools.partial(reduce_side, index))

    def poll(at):
        for event in plan[at]:
            event()

    lane = lax.broadcasted_iota(jnp.int32, (1, length), 1)

    def back(seq):
        turned = mixed_ref[seq_rows(seq), :].astype(F32).T
        mixed_turned[0] = turned.astype(BF16)
        mixed_turned[1] = (turned * turned_sign).astype(BF16)
        for i in range(z.chunks):
            q = (2 + seq) * z.chunks + i
            j, g = i // steps, i % steps
            mixer_load(q).wait()

            def project(k, carry):
                result = dot(mixer_ref[q % 2, aligned(k, width), :], mixed_turned[j]).astype(BF16)
                grad_conv_ref[:, aligned(k, length)] = result
                return carry

            lax.fori_loop(0, z.group, project, 0)
            if q + 2 < 4 * z.chunks:
                mixer_load(q + 2).start()
            taps = toeplitz_ref[g * z.group : (g + 1) * z.group].reshape(z.group * length, length)
            product = dot(grad_conv_ref[...], taps)
            back_ref[j] = product if g == 0 else back_ref[j] + product
            if seq == 0 and i == 1:
                nonlocal gain_two
                gain_two = gain_two + mixed_gradient(1)
            poll(seq * z.chunks + i)
        part_three[seq, across] = (back_ref[0] + turned_sign * back_ref[1]).astype(BF16)
        exchange_three.start(seq)

    for seq in range(z.seqs):
        back(seq)

    for step in range(1, z.dp):
        turn_copy(step).wait()
    turn_mine.wait()
    slots = z.dp
    for slot in range(slots):
        own_rows = slice(slot * z.slice, (slot + 1) * z.slice)
        normed = turned_ref[slot].astype(F32)
        signed_turned[0, own_rows, :] = turned_ref[slot]
        signed_turned[1, own_rows, :] = (normed * turned_sign).astype(BF16)
        conv = (conv_ref, conv_near)[slot // (2 * lines)]
        cols = slice(slot % (2 * lines) * length, (slot % (2 * lines) + 1) * length)
        for lag in range(ORDER):
            shifted = jnp.where(lane >= lag, pltpu.roll(normed, lag, 1), 0.0) if lag else normed
            at = 2 * z.pair_rows + lag * z.slice
            conv[at : at + z.slice, cols] = shifted.astype(BF16)
    half_length = length // 2
    tap_row = lax.broadcasted_iota(jnp.int32, (half_length, length), 0)
    tap_lane = lax.broadcasted_iota(jnp.int32, (half_length, length), 1)

    def convolve_slice(k, carry):
        values = jnp.broadcast_to(plain_rows_ref[pl.ds((across - across % 2) * own + k, 1), :], (half_length, length))
        upper = jnp.where(tap_lane >= tap_row, pltpu.roll(values, 0, 1, stride=1, stride_axis=0), 0.0)
        lower = jnp.concatenate([jnp.zeros((half_length, half_length), F32), upper[:, :half_length]], axis=1)
        taps = jnp.concatenate([upper, lower], axis=0).astype(BF16)
        first = (k // own) * z.pair_rows + (k % own) * z.slice
        for j in range(2):
            result = dot(signed_turned[j], taps)
            if j:
                result = result * turned_sign
            result = result.astype(BF16)
            at = pl.ds(pl.multiple_of(first + j * own * z.slice, z.slice), z.slice)
            for slot in range(slots):
                conv = (conv_ref, conv_near)[slot // (2 * lines)]
                cols = slice(slot % (2 * lines) * length, (slot % (2 * lines) + 1) * length)
                conv[at, cols] = result[slot * z.slice : (slot + 1) * z.slice, :]
        return carry

    for quarter in range(4):
        lax.fori_loop(quarter * 2 * own // 4, (quarter + 1) * 2 * own // 4, convolve_slice, 0)
        poll(2 * z.chunks + quarter)

    def pair_copy(part):
        return pltpu.make_async_remote_copy(
            src_ref=pair_send.at[part],
            dst_ref=pair_recv.at[part],
            send_sem=pair_send_sem.at[part],
            recv_sem=pair_recv_sem.at[part],
            device_id=(me, partner),
            device_id_type=MESH,
        )

    blocks = [slice(0, z.pair_rows), slice(z.pair_rows, 2 * z.pair_rows), slice(2 * z.pair_rows, z.all_rows)]
    for part in range(2):
        cols = slice(part * half, (part + 1) * half)
        for far in range(2):
            await_core(part, far)
            tokens = slice(far * z.near, (far + 1) * z.near)
            conv = (conv_ref, conv_near)[far]
            for taken in blocks:
                product = dot(conv[taken, : z.near], gathered[part, tokens, :])
                sum_ref[taken, cols] = product if far == 0 else sum_ref[taken, cols] + product
        pair_send[part, : z.pair_rows, :] = sum_ref[aligned(1 - across % 2, z.pair_rows), cols].astype(BF16)
        pair_send[part, z.pair_rows :, :] = sum_ref[2 * z.pair_rows : z.all_rows, cols].astype(BF16)
        pair_copy(part).start()

    for seq in range(z.seqs):
        turned = mixed_ref[seq_rows(seq), :].astype(F32).T
        total = dot(ar_ref[:width, :], turned.astype(BF16))
        for lag in range(1, ORDER):
            shifted = jnp.where(lane < length - lag, pltpu.roll(turned, length - lag, 1), 0.0).astype(BF16)
            total = total + dot(ar_ref[lag * width : (lag + 1) * width, :], shifted)
        ar_back_ref[seq] = total
    gain_one = jnp.zeros((1, width), F32)
    for seq in range(z.seqs):
        exchange_three.wait(seq)
        grad = (exchange_three.total(seq, ()) + ar_back_ref[seq]).T
        own_rows = seq_rows(seq)
        values = x_ref[own_rows, :].astype(F32)
        scale = rms_scale(values)
        normed = values * scale
        gain_one = gain_one + jnp.sum(grad * normed, axis=0, keepdims=True)
        weighted = grad * gain_one_ref[...]
        input_grad_ref[own_rows, :] += scale * (
            weighted - normed * jnp.mean(weighted * normed, axis=-1, keepdims=True)
        )
    gains[me] = jnp.concatenate([gain_two, gain_one, jnp.zeros((6, width), F32)], axis=0)

    def gain_copy(step):
        return pltpu.make_async_remote_copy(
            src_ref=gains.at[me],
            dst_ref=gains.at[me],
            send_sem=gain_send.at[step - 1],
            recv_sem=gain_recv.at[step - 1],
            device_id=((me + step) % z.dp, across),
            device_id_type=MESH,
        )

    for step in range(1, z.dp):
        gain_copy(step).start()
    writes = [write(input_grad_ref, input_grad_hbm, 0)]

    for seq in range(z.seqs):
        exchange_out.wait(seq)
        output_ref[seq_rows(seq), :] += exchange_out.total(seq, ())
    writes.append(write(output_ref, output_hbm, 1))

    for index in range(3):
        total = ring_side[index, line].astype(F32)
        for step in range(1, lines):
            line_copy(index, step).wait()
            total = total + ring_line[index, step - 1].astype(F32)
        weight_grad_ref[index] = total
    writes.append(write(weight_grad_ref, weight_grad_hbm, 2))

    for step in range(1, z.dp):
        gain_copy(step).wait()
    gain_grad_ref[...] = functools.reduce(jnp.add, [gains[index] for index in range(z.dp)])
    writes.append(write(gain_grad_ref, gain_grad_hbm, 3))

    mine = aligned(across % 2, z.pair_rows)
    for part in range(2):
        cols = slice(part * half, (part + 1) * half)
        pair_copy(part).wait()
        sum_ref[mine, cols] += pair_recv[part, : z.pair_rows, :].astype(F32)
        ar_grad_ref[:, cols] = pair_send[part, z.pair_rows :, :].astype(F32) + pair_recv[
            part, z.pair_rows :, :
        ].astype(F32)
    writes.append(write(sum_ref.at[mine, :], mixer_grad_hbm, 4))
    writes.append(write(ar_grad_ref, ar_grad_hbm, 5))

    for part in range(2):
        for away in range(lines):
            line_round(part, away, finish_copy)
            side_round(part, away, finish_copy)
    for copy in writes:
        copy.wait()


def finish_kernel(z, gains_ref, *refs):
    sources, targets, (gain_one_out, gain_two_out) = refs[:5], refs[5:12], refs[12:14]
    held, (read_sem, write_sem) = refs[14:19], refs[19:]
    reads = [pltpu.make_async_copy(*pair, read_sem.at[index]) for index, pair in enumerate(zip(sources, held))]
    for read in reads:
        read.start()
    first = lax.axis_index("dp") * z.slice
    rolled = pltpu.roll(gains_ref[...], (z.width - first) % z.width, 1)
    gain_two_out[...] = rolled[0:1, : z.slice]
    gain_one_out[...] = rolled[1:2, : z.slice]
    parts = [*held[:4], *(held[4].at[index] for index in range(3))]
    writes = [pltpu.make_async_copy(*pair, write_sem.at[index]) for index, pair in enumerate(zip(parts, targets))]
    for index, write in enumerate(writes):
        if index < len(reads):
            reads[index].wait()
        write.start()
    for write in writes:
        write.wait()


VMEM_SPEC = pl.BlockSpec(memory_space=pltpu.VMEM)
HBM_SPEC = pl.BlockSpec(memory_space=pl.ANY)
SMEM_SPEC = pl.BlockSpec(memory_space=pltpu.SMEM)
DMA = pltpu.SemaphoreType.DMA


def shape(dims, dtype=F32):
    return jax.ShapeDtypeStruct(dims, dtype)


def low(*dims):
    return pltpu.VMEM(dims, BF16)


def wide(*dims):
    return pltpu.VMEM(dims, F32)


def body(
    mesh_shape,
    inputs,
    cotangent,
    group_ids,
    group_weights,
    filters,
    gain_mixer,
    mixer_weights,
    ar_weights,
    gain_mlp,
    w_gate,
    w_up,
    w_down,
):
    z = Sizes(mesh_shape, inputs.shape, mixer_weights.shape, filters.T.shape, w_gate.shape)
    length, width, rows, half, lines = z.length, z.width, z.rows, z.half, z.line
    others, far_lines = z.tensor - 1, max(1, lines - 1)
    grads = (
        shape((rows, width)),
        shape((rows, width)),
        shape((z.pair_rows, width)),
        shape((z.ar_rows, width)),
        shape((3, z.slice, z.hidden)),
    )
    output, input_grad, mixer_grad, ar_grad, weight_grads, gains = pl.pallas_call(
        functools.partial(block_kernel, z),
        name="block",
        out_shape=(*grads, shape((8, width))),
        in_specs=[SMEM_SPEC] * 2 + [VMEM_SPEC] * 5 + [HBM_SPEC] * 5,
        out_specs=(HBM_SPEC,) * 6,
        scratch_shapes=[
            wide(rows, width),
            wide(rows, width),
            wide(z.ar_rows, width),
            wide(3, z.slice, z.hidden),
            wide(8, width),
            low(2, z.depth, width),
            low(ORDER * width, width),
            low(width, z.hidden),
            low(width, z.hidden),
            low(z.hidden, width),
            low(z.seqs, length, 2 * width),
            low(rows, ORDER * width),
            low(z.dp, z.slice, length),
            low(z.dp, z.slice, length),
            low(2, z.dp * z.slice, length),
            wide(z.filters, length),
            wide(z.filters, length),
            low(z.own, length, length),
            low(z.all_rows, z.near),
            low(max(z.all_rows, z.chunks * length), max(z.near, z.depth)),
            wide(max(z.all_rows, 2 * length), width),
            low(rows, width),
            low(rows, width),
            low(rows, z.hidden),
            low(rows, z.hidden),
            low(rows, z.hidden),
            low(rows, width),
            low(2, width, length),
            low(width, z.group * length),
            wide(2, width, length),
            wide(z.seqs, width, length),
            low(2, z.dp * length, half),
            low(z.seqs, z.tensor, length, width),
            low(z.seqs, z.tensor, length, width),
            low(z.seqs, z.tensor, width, length),
            low(z.seqs, z.tensor, length, width),
            low(2, z.pair_rows + z.ar_rows, half),
            low(2, z.pair_rows + z.ar_rows, half),
            low(3, lines, 2, 2, z.slice, z.hidden),
            low(3, lines, 2, z.slice, z.hidden),
            low(3, lines, z.slice, z.hidden),
            low(3, far_lines, z.slice, z.hidden),
            wide(z.dp, 8, width),
            DMA((2,)),
            DMA((4,)),
            DMA((6,)),
            DMA,
            DMA((z.dp - 1,)),
            DMA((z.dp - 1,)),
            *[DMA((z.seqs, others))] * 8,
            DMA((2, lines, 2, 3)),
            DMA((2, lines, 2)),
            DMA((2, z.dp)),
            *[DMA((3,))] * 4,
            DMA((3, far_lines)),
            DMA((3, far_lines)),
            DMA((2,)),
            DMA((2,)),
            DMA((z.dp - 1,)),
            DMA((z.dp - 1,)),
        ],
        compiler_params=pltpu.CompilerParams(collective_id=1, has_side_effects=True, vmem_limit_bytes=63 * MIB),
    )(
        group_ids,
        group_weights,
        inputs.reshape(rows, width),
        cotangent.reshape(rows, width),
        filters.T,
        gain_mixer.reshape(1, width),
        gain_mlp.reshape(1, width),
        mixer_weights.reshape(2 * z.own * width, width),
        ar_weights.reshape(ORDER * width, width),
        w_gate,
        w_up,
        w_down,
    )
    (
        output,
        input_grad,
        mixer_grad,
        ar_grad,
        gate_grad,
        up_grad,
        down_grad,
        gain_one,
        gain_two,
    ) = pl.pallas_call(
        functools.partial(finish_kernel, z),
        name="finish",
        out_shape=(*grads[:4], *[shape((z.slice, z.hidden))] * 3, *[shape((1, z.slice))] * 2),
        in_specs=[VMEM_SPEC] + [HBM_SPEC] * 5,
        out_specs=(HBM_SPEC,) * 7 + (VMEM_SPEC,) * 2,
        scratch_shapes=[*[pltpu.VMEM(grad.shape, F32) for grad in grads], DMA((5,)), DMA((7,))],
    )(gains, output, input_grad, mixer_grad, ar_grad, weight_grads)
    return (
        output.reshape(inputs.shape),
        input_grad.reshape(inputs.shape),
        gain_one.reshape(z.slice),
        mixer_grad.reshape(2, z.own, z.slice, width),
        ar_grad.reshape(ORDER, z.slice, width),
        gain_two.reshape(z.slice),
        gate_grad,
        up_grad,
        down_grad.T,
    )


def solution(mesh):
    placed = (
        P("dp", None, None),
        P("dp", None, None),
        P("dp"),
        P(),
        P(),
        P(),
        P(None, "tensor", None, None),
        P(),
        P(),
        P(None, "tensor"),
        P(None, "tensor"),
        P("tensor", None),
    )
    return jax.shard_map(
        functools.partial(body, dict(mesh.shape)),
        mesh=mesh,
        in_specs=placed,
        out_specs=(
            P("dp", None, None),
            P("dp", None, None),
            P("dp"),
            P(None, "tensor", "dp", None),
            P(None, "dp", None),
            P("dp"),
            P("dp", "tensor"),
            P("dp", "tensor"),
            P("tensor", "dp"),
        ),
        check_vma=False,
    )
```

```python
import functools

import jax
import jax.numpy as jnp
from jax import lax
from jax.experimental import pallas as pl
from jax.experimental.pallas import tpu as pltpu
from jax.sharding import PartitionSpec as P

F32 = jnp.float32
BF16 = jnp.bfloat16
MESH = pl.DeviceIdType.MESH
EPSILON = 1e-06
ROOT_HALF = 0.7071067811865476
INV_ROOT_TWO_PI = 0.3989422804014327
ORDER = 3
MIB = 2**20


def dot(left, right):
    return jnp.dot(left, right, preferred_element_type=F32)


def dot_cols(left, right):
    return lax.dot_general(left, right, (((1,), (1,)), ((), ())), preferred_element_type=F32)


def dot_rows(left, right):
    return lax.dot_general(left, right, (((0,), (0,)), ((), ())), preferred_element_type=F32)


def rms_scale(values):
    return lax.rsqrt(jnp.mean(values * values, axis=-1, keepdims=True) + EPSILON)


def row_sign(rows):
    odd = lax.broadcasted_iota(jnp.int32, (rows, 1), 0) % 2
    return 1.0 - 2.0 * odd.astype(F32)


def lane_sign(lanes):
    odd = lax.broadcasted_iota(jnp.int32, (1, lanes), 1) % 2
    return 1.0 - 2.0 * odd.astype(F32)


def aligned(index, step):
    return pl.ds(pl.multiple_of(index * step, step), step)


class Sizes:
    def __init__(self, mesh_shape, inputs, mixer_weights, filters, w_gate):
        self.seqs, self.length, self.width = inputs
        self.rows = self.seqs * self.length
        self.dp = mesh_shape["dp"]
        self.tensor = mesh_shape["tensor"]
        self.line = self.dp // 4
        self.own = mixer_weights[1]
        self.filters = filters[0]
        self.hidden = w_gate[1]
        self.slice = self.width // self.dp
        self.group = max(g for g in range(1, 5) if self.own % g == 0)
        self.depth = self.group * self.width
        self.chunks = 2 * self.own // self.group
        self.half = self.width // 2
        self.near = self.dp // 2 * self.length
        self.pair_rows = 2 * self.own * self.slice
        self.ar_rows = ORDER * self.slice
        self.all_rows = 2 * self.pair_rows + self.ar_rows


def place(z):
    dp = lax.axis_index("dp")
    return dp // 4, (dp // 2) % 2, dp % 2, lax.axis_index("tensor")


def dp_of(line, side, core):
    return (line * 2 + side) * 2 + core


def reversed_rows(filters_ref):
    length = filters_ref.shape[1]
    source = lax.broadcasted_iota(jnp.int32, (length, length), 0)
    target = lax.broadcasted_iota(jnp.int32, (length, length), 1)
    pick = (source == (length + length // 2 - target) % length).astype(BF16)
    return dot(filters_ref[...], pick)


def toeplitz_own(z, own_first, rows_ref, out_ref):
    length, half = z.length, z.length // 2
    lane = lax.broadcasted_iota(jnp.int32, (half, length), 1)
    row = lax.broadcasted_iota(jnp.int32, (half, length), 0)

    def step(k, carry):
        values = jnp.broadcast_to(rows_ref[pl.ds(own_first + k, 1), :], (half, length))
        rolled = pltpu.roll(values, 0, 1, stride=1, stride_axis=0)
        lower = jnp.where(lane <= row + half, rolled, 0.0).astype(BF16)
        out_ref[k, half:, :] = lower
        out_ref[k, :half, :half] = lower[:, half:]
        out_ref[k, :half, half:] = jnp.zeros((half, half), BF16)
        return carry

    lax.fori_loop(0, z.own, step, 0)


def shared_copy(buffer, slot, send, recv, peer):
    return pltpu.make_async_remote_copy(
        src_ref=buffer.at[slot],
        dst_ref=buffer.at[slot],
        send_sem=send,
        recv_sem=recv,
        device_id=(lax.axis_index("dp"), peer),
        device_id_type=MESH,
    )


class Exchange:
    def __init__(self, z, buffer, send, recv):
        self.z, self.buffer, self.send, self.recv = z, buffer, send, recv

    def copies(self, part):
        me = lax.axis_index("tensor")
        return [
            shared_copy(
                self.buffer.at[part],
                me,
                self.send.at[part, step - 1],
                self.recv.at[part, step - 1],
                (me + step) % self.z.tensor,
            )
            for step in range(1, self.z.tensor)
        ]

    def start(self, part):
        for copy in self.copies(part):
            copy.start()

    def wait(self, part):
        for copy in self.copies(part):
            copy.wait()

    def total(self, part, where):
        terms = [self.buffer[(part, peer) + where].astype(F32) for peer in range(self.z.tensor)]
        return functools.reduce(jnp.add, terms)


def block_kernel(
    z,
    ids_ref,
    group_ref,
    x_ref,
    cotangent_ref,
    filters_ref,
    gain_one_ref,
    gain_two_ref,
    mixer_hbm,
    ar_hbm,
    gate_hbm,
    up_hbm,
    down_hbm,
    output_hbm,
    input_grad_hbm,
    mixer_grad_hbm,
    ar_grad_hbm,
    weight_grad_hbm,
    gain_grad_hbm,
    output_ref,
    input_grad_ref,
    ar_grad_ref,
    weight_grad_ref,
    gain_grad_ref,
    mixer_ref,
    ar_ref,
    gate_ref,
    up_ref,
    down_ref,
    signed_ref,
    lagged_ref,
    turned_mine,
    turned_ref,
    signed_turned,
    rows_ref,
    plain_rows_ref,
    toeplitz_ref,
    conv_ref,
    conv_near,
    sum_ref,
    normed_two_ref,
    low_ref,
    active_ref,
    gate_pre_ref,
    up_pre_ref,
    mixed_ref,
    mixed_turned,
    grad_conv_ref,
    back_ref,
    ar_back_ref,
    gathered,
    part_one,
    part_two,
    part_three,
    part_out,
    pair_send,
    pair_recv,
    grads_ref,
    ring_core,
    ring_side,
    ring_line,
    gains,
    mixer_sem,
    load_sem,
    write_sem,
    turn_own,
    turn_send,
    turn_recv,
    one_send,
    one_recv,
    two_send,
    two_recv,
    three_send,
    three_recv,
    out_send,
    out_recv,
    gather_send,
    gather_side_send,
    gather_recv,
    core_send,
    core_recv,
    side_send,
    side_recv,
    line_send,
    line_recv,
    pair_send_sem,
    pair_recv_sem,
    gain_send,
    gain_recv,
):
    line, side, core, across = place(z)
    me = lax.axis_index("dp")
    length, width, rows, half = z.length, z.width, z.rows, z.half
    lines, own, steps = z.line, z.own, z.own // z.group
    other = dp_of(line, side, 1 - core)
    opposite = dp_of(line, 1 - side, core)
    partner = across + 1 - 2 * (across % 2)
    own_seq = (across + core) % 2

    def mixer_load(q):
        slot = q % 3
        source = mixer_hbm.at[aligned(q % z.chunks, z.depth), :]
        return pltpu.make_async_copy(source, mixer_ref.at[slot], mixer_sem.at[slot])

    loads = [
        pltpu.make_async_copy(source, target, load_sem.at[index])
        for index, (source, target) in enumerate(
            ((ar_hbm, ar_ref), (gate_hbm, gate_ref), (up_hbm, up_ref), (down_hbm, down_ref))
        )
    ]
    mixer_load(0).start()
    mixer_load(1).start()
    mixer_load(2).start()

    barrier = pltpu.get_barrier_semaphore()
    for step in range(1, z.tensor):
        pl.semaphore_signal(barrier, inc=1, device_id=(me, (across + step) % z.tensor), device_id_type=MESH)
    for step in range(1, z.dp):
        pl.semaphore_signal(barrier, inc=1, device_id=((me + step) % z.dp, across), device_id_type=MESH)

    sign = row_sign(length)
    turned_sign = lane_sign(length)
    for seq in range(z.seqs):
        values = x_ref[seq * length : (seq + 1) * length, :].astype(F32)
        normed = (values * rms_scale(values) * gain_one_ref[...]).astype(BF16)
        signed_ref[seq, :, :width] = normed
        signed_ref[seq, :, width:] = (normed.astype(F32) * sign).astype(BF16)
    rows_ref[...] = reversed_rows(filters_ref)
    plain_rows_ref[...] = filters_ref[...].astype(F32)
    toeplitz_own(z, across * own, rows_ref, toeplitz_ref)

    exchange_one = Exchange(z, part_one, one_send, one_recv)
    exchange_two = Exchange(z, part_two, two_send, two_recv)
    exchange_three = Exchange(z, part_three, three_send, three_recv)
    exchange_out = Exchange(z, part_out, out_send, out_recv)

    def seq_rows(seq):
        return slice(seq * length, (seq + 1) * length)

    def mix(seq):
        def convolve(k, carry):
            result = dot(toeplitz_ref[k], signed_ref[seq]).astype(BF16)
            for j in range(2):
                chunk = j * steps + k // z.group
                conv_near[aligned(chunk, length), aligned(k % z.group, width)] = result[:, j * width : (j + 1) * width]
            return carry

        lax.fori_loop(0, own, convolve, 0, unroll=2)
        if seq == 0:
            for load in loads:
                load.start()
        sum_ref[: 2 * length, :] = jnp.zeros((2 * length, width), F32)

        def project(i, carry):
            q = seq * z.chunks + i
            mixer_load(q).wait()
            sum_ref[aligned(i // steps, length), :] += dot(conv_near[aligned(i, length), : z.depth], mixer_ref[q % 3])
            mixer_load(q + 3).start()
            return carry

        lax.fori_loop(0, z.chunks, project, 0)
        part_one[seq, across] = (sum_ref[:length, :] + sign * sum_ref[length : 2 * length, :]).astype(BF16)

    mix(0)
    pl.semaphore_wait(barrier, z.dp - 1 + z.tensor - 1)
    exchange_one.start(0)

    turned_mine[...] = signed_ref[own_seq, :, :width].astype(F32).T.astype(BF16).reshape(z.dp, z.slice, length)

    def turn_copy(step):
        peer = (me + step) % z.dp
        far = (side + (peer // 2) % 2) % 2
        return pltpu.make_async_remote_copy(
            src_ref=turned_mine.at[peer],
            dst_ref=turned_ref.at[far * (2 * lines) + line * 2 + core],
            send_sem=turn_send.at[step - 1],
            recv_sem=turn_recv.at[step - 1],
            device_id=(peer, across),
            device_id_type=MESH,
        )

    for step in range(1, z.dp):
        turn_copy(step).start()
    turn_mine = pltpu.make_async_copy(turned_mine.at[me], turned_ref.at[line * 2 + core], turn_own)
    turn_mine.start()

    mix(1)
    exchange_one.start(1)

    row = lax.broadcasted_iota(jnp.int32, (length, 1), 0)
    loads[0].wait()
    scales = []
    for seq in range(z.seqs):
        own_rows = seq_rows(seq)
        normed = signed_ref[seq, :, :width].astype(F32)
        for lag in range(ORDER):
            shifted = jnp.where(row >= lag, pltpu.roll(normed, lag, 0), 0.0) if lag else normed
            lagged_ref[own_rows, lag * width : (lag + 1) * width] = shifted.astype(BF16)
        scale = jnp.int32(0)
        for group in range(group_ref.shape[0]):
            scale = scale + jnp.where(ids_ref[seq] == group, group_ref[group], 0)
        scales.append(scale.astype(F32))
        low_ref[own_rows, :] = (cotangent_ref[own_rows, :].astype(F32) * scales[seq]).astype(BF16)
    output_ref[...] = dot(lagged_ref[...], ar_ref[...])

    chunk = min(256, z.hidden)

    def feed_forward(seq):
        own_rows = seq_rows(seq)
        exchange_one.wait(seq)
        for start in range(seq * length, (seq + 1) * length, 128):
            block = slice(start, start + 128)
            inside = slice(start - seq * length, start - seq * length + 128)
            hidden = x_ref[block, :].astype(F32) + (exchange_one.total(seq, (inside,)) + output_ref[block, :])
            output_ref[block, :] = hidden
            normed_two_ref[block, :] = (hidden * rms_scale(hidden) * gain_two_ref[...]).astype(BF16)
        if seq == 0:
            for load in loads[1:]:
                load.wait()

        def feed(c, carry):
            units = aligned(c, chunk)
            gate = dot(normed_two_ref[own_rows, :], gate_ref[:, units])
            up = dot(normed_two_ref[own_rows, :], up_ref[:, units])
            cdf = 0.5 * (1.0 + lax.erf(gate * ROOT_HALF))
            activated = gate * cdf
            active_ref[own_rows, units] = (activated * up).astype(BF16)
            grad = dot_cols(low_ref[own_rows, :], down_ref[units, :])
            density = jnp.exp(-0.5 * gate * gate) * INV_ROOT_TWO_PI
            gate_pre_ref[own_rows, units] = (grad * up * (cdf + gate * density)).astype(BF16)
            up_pre_ref[own_rows, units] = (grad * activated).astype(BF16)
            return carry

        lax.fori_loop(0, z.hidden // chunk, feed, 0)
        grad = dot_cols(gate_pre_ref[own_rows, :], gate_ref[...]) + dot_cols(up_pre_ref[own_rows, :], up_ref[...])
        part_two[seq, across] = grad.astype(BF16)
        exchange_two.start(seq)

    for seq in range(z.seqs):
        feed_forward(seq)

    def core_copy(index):
        return pltpu.make_async_remote_copy(
            src_ref=grads_ref.at[index, :, :, 1 - core],
            dst_ref=ring_core.at[index],
            send_sem=core_send.at[index],
            recv_sem=core_recv.at[index],
            device_id=(other, across),
            device_id_type=MESH,
        )

    for index, (left, right) in enumerate(
        ((normed_two_ref, gate_pre_ref), (normed_two_ref, up_pre_ref), (low_ref, active_ref))
    ):
        product = dot_rows(left[...], right[...]).astype(BF16)
        grads_ref[index] = product.reshape(lines, 2, 2, z.slice, z.hidden)
        core_copy(index).start()
    for seq in range(z.seqs):
        part_out[seq, across] = dot(active_ref[seq_rows(seq), :], down_ref[...]).astype(BF16)

    def slot_of(far, at):
        return far * (2 * lines) + at * 2 + core

    def gather_copy(part, source, target, send, peer):
        return pltpu.make_async_remote_copy(
            src_ref=gathered.at[part, aligned(source, length), :],
            dst_ref=gathered.at[part, aligned(target, length), :],
            send_sem=send,
            recv_sem=gather_recv.at[part, target],
            device_id=(peer, across),
            device_id_type=MESH,
        )

    def line_block(part, away, up):
        at = line - away if up else line + away
        slot = slot_of(0, at)
        sems = gather_send.at[part, away, up]
        onward = dp_of(jnp.clip(line + (1 if up else -1), 0, lines - 1), side, core)
        return (
            jnp.logical_and(at >= 0, at < lines),
            lambda: gather_copy(part, slot, slot_of(1, at), sems.at[0], opposite),
            lambda: gather_copy(part, slot, slot, sems.at[1], other),
            lambda: gather_copy(part, slot, slot, sems.at[2], onward),
        )

    def has_onward(up):
        return line + 1 < lines if up else line >= 1

    def start_copy(copy):
        copy.start()

    def finish_copy(copy):
        copy.wait_send()

    def line_round(part, away, act):
        if away == 0:
            _, to_side, to_core, to_line = line_block(part, 0, 1)
            _, _, _, down_line = line_block(part, 0, 0)
            pl.when(has_onward(1))(lambda: act(to_line()))
            pl.when(has_onward(0))(lambda: act(down_line()))
            act(to_side())
            act(to_core())
            return
        for up in (1, 0):
            there, to_side, to_core, to_line = line_block(part, away, up)

            def pass_on(to_side=to_side, to_core=to_core, to_line=to_line, up=up):
                if act is start_copy:
                    to_core().wait_recv()
                pl.when(has_onward(up))(lambda: act(to_line()))
                act(to_side())
                act(to_core())

            pl.when(there)(pass_on)

    def side_round(part, away, act):
        for up in (1, 0) if away else (1,):
            at = line - away if up else line + away

            def pass_on(at=at, up=up):
                slot = slot_of(1, at)
                copy = gather_copy(part, slot, slot, gather_side_send.at[part, away, up], other)
                if act is start_copy:
                    copy.wait_recv()
                act(copy)

            pl.when(jnp.logical_and(at >= 0, at < lines))(pass_on)

    def await_core(part, far):
        for at in range(lines):
            slot = far * (2 * lines) + at * 2 + 1 - core
            gather_copy(part, slot, slot, gather_side_send.at[part, 0, 0], other).wait_recv()

    def mixed_gradient(seq):
        exchange_two.wait(seq)
        gain = jnp.zeros((1, width), F32)
        for start in range(seq * length, (seq + 1) * length, 128):
            block = slice(start, start + 128)
            inside = slice(start - seq * length, start - seq * length + 128)
            grad = exchange_two.total(seq, (inside,))
            hidden = output_ref[block, :]
            scale = rms_scale(hidden)
            normed = hidden * scale
            gain = gain + jnp.sum(grad * normed, axis=0, keepdims=True)
            weighted = grad * gain_two_ref[...]
            upstream = cotangent_ref[block, :].astype(F32) * scales[seq]
            grad_hidden = upstream + scale * (weighted - normed * jnp.mean(weighted * normed, axis=-1, keepdims=True))
            input_grad_ref[block, :] = grad_hidden
            mixed_ref[block, :] = grad_hidden.astype(BF16)

        def send():
            for part in range(2):
                gathered[part, aligned(slot_of(0, line), length), :] = mixed_ref[
                    seq_rows(seq), part * half : (part + 1) * half
                ]
            line_round(0, 0, start_copy)

        pl.when(own_seq == seq)(send)
        return gain

    def side_copy(index):
        return pltpu.make_async_remote_copy(
            src_ref=grads_ref.at[index, :, 1 - side, core],
            dst_ref=ring_side.at[index],
            send_sem=side_send.at[index],
            recv_sem=side_recv.at[index],
            device_id=(opposite, across),
            device_id_type=MESH,
        )

    def reduce_core(index):
        core_copy(index).wait()
        for at in range(lines):
            for where in range(2):
                grads_ref[index, at, where, core] = (
                    grads_ref[index, at, where, core].astype(F32) + ring_core[index, at, where].astype(F32)
                ).astype(BF16)
        side_copy(index).start()

    def line_copy(index, step):
        target = (line + step) % lines
        return pltpu.make_async_remote_copy(
            src_ref=ring_side.at[index, target],
            dst_ref=ring_line.at[index, step - 1],
            send_sem=line_send.at[index, step - 1],
            recv_sem=line_recv.at[index, step - 1],
            device_id=(dp_of(target, side, core), across),
            device_id_type=MESH,
        )

    def reduce_side(index):
        side_copy(index).wait()
        for at in range(lines):
            ring_side[index, at] = (
                ring_side[index, at].astype(F32) + grads_ref[index, at, side, core].astype(F32)
            ).astype(BF16)
        for step in range(1, lines):
            line_copy(index, step).start()

    def write(source, target, index):
        copy = pltpu.make_async_copy(source, target, write_sem.at[index])
        copy.start()
        return copy

    second = 4 + z.chunks + 2
    positions = second + z.chunks + 2
    plan = {at: [] for at in range(positions)}

    def at_position(at, last, event, *args):
        plan[min(at, last)].append(functools.partial(event, *args))

    for late in range(2):

        def when_own(event, *args, late=late):
            pl.when(own_seq == late)(functools.partial(event, *args))

        first = 2 * late
        for part in range(2):
            last = (second - 3, positions - 3)[part]
            if part:
                at_position(first, last, when_own, line_round, part, 0, start_copy)
            for away in range(1, lines):
                at_position(first + part + away - 1, last, when_own, line_round, part, away, start_copy)
                at_position(first + part + away, last, when_own, side_round, part, away - 1, start_copy)
            at_position(first + part + lines, last, when_own, side_round, part, lines - 1, start_copy)
    for index in range(3):
        at_position(5 + index, positions - 1, reduce_core, index)
        at_position(second - 1 + 2 * index, positions - 1, reduce_side, index)

    def poll(at):
        for event in plan[at]:
            event()

    gain_two = mixed_gradient(0)
    lane = lax.broadcasted_iota(jnp.int32, (1, length), 1)

    for step in range(1, z.dp):
        turn_copy(step).wait()
    turn_mine.wait()
    slots = z.dp
    for slot in range(slots):
        own_rows = slice(slot * z.slice, (slot + 1) * z.slice)
        normed = turned_ref[slot].astype(F32)
        signed_turned[0, own_rows, :] = turned_ref[slot]
        signed_turned[1, own_rows, :] = (normed * turned_sign).astype(BF16)
        conv = (conv_ref, conv_near)[slot // (2 * lines)]
        cols = slice(slot % (2 * lines) * length, (slot % (2 * lines) + 1) * length)
        for lag in range(ORDER):
            shifted = jnp.where(lane >= lag, pltpu.roll(normed, lag, 1), 0.0) if lag else normed
            at = 2 * z.pair_rows + lag * z.slice
            conv[at : at + z.slice, cols] = shifted.astype(BF16)
    half_length = length // 2
    tap_row = lax.broadcasted_iota(jnp.int32, (half_length, length), 0)
    tap_lane = lax.broadcasted_iota(jnp.int32, (half_length, length), 1)

    def convolve_slice(k, carry):
        values = jnp.broadcast_to(plain_rows_ref[pl.ds((across - across % 2) * own + k, 1), :], (half_length, length))
        upper = jnp.where(tap_lane >= tap_row, pltpu.roll(values, 0, 1, stride=1, stride_axis=0), 0.0)
        lower = jnp.concatenate([jnp.zeros((half_length, half_length), F32), upper[:, :half_length]], axis=1)
        taps = jnp.concatenate([upper, lower], axis=0).astype(BF16)
        first = (k // own) * z.pair_rows + (k % own) * z.slice
        for j in range(2):
            result = dot(signed_turned[j], taps)
            if j:
                result = result * turned_sign
            result = result.astype(BF16)
            at = pl.ds(pl.multiple_of(first + j * own * z.slice, z.slice), z.slice)
            for slot in range(slots):
                conv = (conv_ref, conv_near)[slot // (2 * lines)]
                cols = slice(slot % (2 * lines) * length, (slot % (2 * lines) + 1) * length)
                conv[at, cols] = result[slot * z.slice : (slot + 1) * z.slice, :]
        return carry

    for quarter in range(4):
        lax.fori_loop(quarter * 2 * own // 4, (quarter + 1) * 2 * own // 4, convolve_slice, 0)
        poll(quarter)
        if quarter == 1:
            gain_two = gain_two + mixed_gradient(1)
            for seq in range(z.seqs):
                exchange_out.start(seq)

    def back(seq):
        turned = mixed_ref[seq_rows(seq), :].astype(F32).T
        mixed_turned[0] = turned.astype(BF16)
        mixed_turned[1] = (turned * turned_sign).astype(BF16)
        for i in range(z.chunks):
            q = (2 + seq) * z.chunks + i
            j, g = i // steps, i % steps
            mixer_load(q).wait()

            def project(k, carry):
                result = dot(mixer_ref[q % 3, aligned(k, width), :], mixed_turned[j]).astype(BF16)
                grad_conv_ref[:, aligned(k, length)] = result
                return carry

            lax.fori_loop(0, z.group, project, 0)
            if q + 3 < 4 * z.chunks:
                mixer_load(q + 3).start()
            taps = toeplitz_ref[g * z.group : (g + 1) * z.group].reshape(z.group * length, length)
            product = dot(grad_conv_ref[...], taps)
            back_ref[j] = product if g == 0 else back_ref[j] + product
            poll((4, second)[seq] + i)
        part_three[seq, across] = (back_ref[0] + turned_sign * back_ref[1]).astype(BF16)
        exchange_three.start(seq)

    def pair_copy(part):
        return pltpu.make_async_remote_copy(
            src_ref=pair_send.at[part],
            dst_ref=pair_recv.at[part],
            send_sem=pair_send_sem.at[part],
            recv_sem=pair_recv_sem.at[part],
            device_id=(me, partner),
            device_id_type=MESH,
        )

    mine, theirs = aligned(across % 2, z.pair_rows), aligned(1 - across % 2, z.pair_rows)
    shared = slice(2 * z.pair_rows, z.all_rows)
    for part in range(2):
        back(part)
        cols = slice(part * half, (part + 1) * half)

        def add_product(taken, far, cols=cols, part=part):
            tokens = slice(far * z.near, (far + 1) * z.near)
            product = dot((conv_ref, conv_near)[far][taken, : z.near], gathered[part, tokens, :])
            sum_ref[taken, cols] = product if far == 0 else sum_ref[taken, cols] + product

        await_core(part, 0)
        for taken in (mine, theirs, shared):
            add_product(taken, 0)
        poll((second, positions)[part] - 2)
        await_core(part, 1)
        for taken in (theirs, shared):
            add_product(taken, 1)
        pair_send[part, : z.pair_rows, :] = sum_ref[theirs, cols].astype(BF16)
        pair_send[part, z.pair_rows :, :] = sum_ref[shared, cols].astype(BF16)
        pair_copy(part).start()
        add_product(mine, 1)
        poll((second, positions)[part] - 1)

    for seq in range(z.seqs):
        turned = mixed_ref[seq_rows(seq), :].astype(F32).T
        total = dot(ar_ref[:width, :], turned.astype(BF16))
        for lag in range(1, ORDER):
            shifted = jnp.where(lane < length - lag, pltpu.roll(turned, length - lag, 1), 0.0).astype(BF16)
            total = total + dot(ar_ref[lag * width : (lag + 1) * width, :], shifted)
        ar_back_ref[seq] = total
    for seq in range(z.seqs):
        exchange_out.wait(seq)
        output_ref[seq_rows(seq), :] += exchange_out.total(seq, ())
    writes = [write(output_ref, output_hbm, 1)]

    gain_one = jnp.zeros((1, width), F32)
    for seq in range(z.seqs):
        exchange_three.wait(seq)
        grad = (exchange_three.total(seq, ()) + ar_back_ref[seq]).T
        own_rows = seq_rows(seq)
        values = x_ref[own_rows, :].astype(F32)
        scale = rms_scale(values)
        normed = values * scale
        gain_one = gain_one + jnp.sum(grad * normed, axis=0, keepdims=True)
        weighted = grad * gain_one_ref[...]
        input_grad_ref[own_rows, :] += scale * (
            weighted - normed * jnp.mean(weighted * normed, axis=-1, keepdims=True)
        )
    gains[me] = jnp.concatenate([gain_two, gain_one], axis=0)

    def gain_copy(step):
        return pltpu.make_async_remote_copy(
            src_ref=gains.at[me],
            dst_ref=gains.at[me],
            send_sem=gain_send.at[step - 1],
            recv_sem=gain_recv.at[step - 1],
            device_id=((me + step) % z.dp, across),
            device_id_type=MESH,
        )

    for step in range(1, z.dp):
        gain_copy(step).start()
    writes.append(write(input_grad_ref, input_grad_hbm, 0))

    for index in range(3):
        total = ring_side[index, line].astype(F32)
        for step in range(1, lines):
            line_copy(index, step).wait()
            total = total + ring_line[index, step - 1].astype(F32)
        weight_grad_ref[index] = total
    writes.append(write(weight_grad_ref, weight_grad_hbm, 2))

    for step in range(1, z.dp):
        gain_copy(step).wait()
    gain_grad_ref[...] = functools.reduce(jnp.add, [gains[index] for index in range(z.dp)])
    writes.append(write(gain_grad_ref, gain_grad_hbm, 3))

    for part in range(2):
        cols = slice(part * half, (part + 1) * half)
        pair_copy(part).wait()
        sum_ref[mine, cols] += pair_recv[part, : z.pair_rows, :].astype(F32)
        ar_grad_ref[:, cols] = pair_send[part, z.pair_rows :, :].astype(F32) + pair_recv[
            part, z.pair_rows :, :
        ].astype(F32)
    writes.append(write(sum_ref.at[mine, :], mixer_grad_hbm, 4))
    writes.append(write(ar_grad_ref, ar_grad_hbm, 5))

    for part in range(2):
        for away in range(lines):
            line_round(part, away, finish_copy)
            side_round(part, away, finish_copy)
    for copy in writes:
        copy.wait()


def finish_kernel(z, gains_ref, *refs):
    sources, targets, (gain_one_out, gain_two_out) = refs[:5], refs[5:12], refs[12:14]
    held, (read_sem, write_sem) = refs[14:19], refs[19:]
    reads = [pltpu.make_async_copy(*pair, read_sem.at[index]) for index, pair in enumerate(zip(sources, held))]
    for read in reads:
        read.start()
    first = lax.axis_index("dp") * z.slice
    rolled = pltpu.roll(gains_ref[...], (z.width - first) % z.width, 1)
    gain_two_out[...] = rolled[0:1, : z.slice]
    gain_one_out[...] = rolled[1:2, : z.slice]
    parts = [*held[:4], *(held[4].at[index] for index in range(3))]
    writes = [pltpu.make_async_copy(*pair, write_sem.at[index]) for index, pair in enumerate(zip(parts, targets))]
    for index, write in enumerate(writes):
        if index < len(reads):
            reads[index].wait()
        write.start()
    for write in writes:
        write.wait()


VMEM_SPEC = pl.BlockSpec(memory_space=pltpu.VMEM)
HBM_SPEC = pl.BlockSpec(memory_space=pl.ANY)
SMEM_SPEC = pl.BlockSpec(memory_space=pltpu.SMEM)
DMA = pltpu.SemaphoreType.DMA


def shape(dims, dtype=F32):
    return jax.ShapeDtypeStruct(dims, dtype)


def low(*dims):
    return pltpu.VMEM(dims, BF16)


def wide(*dims):
    return pltpu.VMEM(dims, F32)


def body(
    mesh_shape,
    inputs,
    cotangent,
    group_ids,
    group_weights,
    filters,
    gain_mixer,
    mixer_weights,
    ar_weights,
    gain_mlp,
    w_gate,
    w_up,
    w_down,
):
    z = Sizes(mesh_shape, inputs.shape, mixer_weights.shape, filters.T.shape, w_gate.shape)
    length, width, rows, half, lines = z.length, z.width, z.rows, z.half, z.line
    others, far_lines = z.tensor - 1, max(1, lines - 1)
    grads = (
        shape((rows, width)),
        shape((rows, width)),
        shape((z.pair_rows, width)),
        shape((z.ar_rows, width)),
        shape((3, z.slice, z.hidden)),
    )
    output, input_grad, mixer_grad, ar_grad, weight_grads, gains = pl.pallas_call(
        functools.partial(block_kernel, z),
        name="block",
        out_shape=(*grads, shape((2, width))),
        in_specs=[SMEM_SPEC] * 2 + [VMEM_SPEC] * 5 + [HBM_SPEC] * 5,
        out_specs=(HBM_SPEC,) * 6,
        scratch_shapes=[
            wide(rows, width),
            wide(rows, width),
            wide(z.ar_rows, width),
            wide(3, z.slice, z.hidden),
            wide(2, width),
            low(3, z.depth, width),
            low(ORDER * width, width),
            low(width, z.hidden),
            low(width, z.hidden),
            low(z.hidden, width),
            low(z.seqs, length, 2 * width),
            low(rows, ORDER * width),
            low(z.dp, z.slice, length),
            low(z.dp, z.slice, length),
            low(2, z.dp * z.slice, length),
            wide(z.filters, length),
            wide(z.filters, length),
            low(z.own, length, length),
            low(z.all_rows, z.near),
            low(max(z.all_rows, z.chunks * length), max(z.near, z.depth)),
            wide(max(z.all_rows, 2 * length), width),
            low(rows, width),
            low(rows, width),
            low(rows, z.hidden),
            low(rows, z.hidden),
            low(rows, z.hidden),
            low(rows, width),
            low(2, width, length),
            low(width, z.group * length),
            wide(2, width, length),
            wide(z.seqs, width, length),
            low(2, z.dp * length, half),
            low(z.seqs, z.tensor, length, width),
            low(z.seqs, z.tensor, length, width),
            low(z.seqs, z.tensor, width, length),
            low(z.seqs, z.tensor, length, width),
            low(2, z.pair_rows + z.ar_rows, half),
            low(2, z.pair_rows + z.ar_rows, half),
            low(3, lines, 2, 2, z.slice, z.hidden),
            low(3, lines, 2, z.slice, z.hidden),
            low(3, lines, z.slice, z.hidden),
            low(3, far_lines, z.slice, z.hidden),
            wide(z.dp, 2, width),
            DMA((3,)),
            DMA((4,)),
            DMA((6,)),
            DMA,
            DMA((z.dp - 1,)),
            DMA((z.dp - 1,)),
            *[DMA((z.seqs, others))] * 8,
            DMA((2, lines, 2, 3)),
            DMA((2, lines, 2)),
            DMA((2, z.dp)),
            *[DMA((3,))] * 4,
            DMA((3, far_lines)),
            DMA((3, far_lines)),
            DMA((2,)),
            DMA((2,)),
            DMA((z.dp - 1,)),
            DMA((z.dp - 1,)),
        ],
        compiler_params=pltpu.CompilerParams(collective_id=1, has_side_effects=True, vmem_limit_bytes=63 * MIB),
    )(
        group_ids,
        group_weights,
        inputs.reshape(rows, width),
        cotangent.reshape(rows, width),
        filters.T,
        gain_mixer.reshape(1, width),
        gain_mlp.reshape(1, width),
        mixer_weights.reshape(2 * z.own * width, width),
        ar_weights.reshape(ORDER * width, width),
        w_gate,
        w_up,
        w_down,
    )
    (
        output,
        input_grad,
        mixer_grad,
        ar_grad,
        gate_grad,
        up_grad,
        down_grad,
        gain_one,
        gain_two,
    ) = pl.pallas_call(
        functools.partial(finish_kernel, z),
        name="finish",
        out_shape=(*grads[:4], *[shape((z.slice, z.hidden))] * 3, *[shape((1, z.slice))] * 2),
        in_specs=[VMEM_SPEC] + [HBM_SPEC] * 5,
        out_specs=(HBM_SPEC,) * 7 + (VMEM_SPEC,) * 2,
        scratch_shapes=[*[pltpu.VMEM(grad.shape, F32) for grad in grads], DMA((5,)), DMA((7,))],
    )(gains, output, input_grad, mixer_grad, ar_grad, weight_grads)
    return (
        output.reshape(inputs.shape),
        input_grad.reshape(inputs.shape),
        gain_one.reshape(z.slice),
        mixer_grad.reshape(2, z.own, z.slice, width),
        ar_grad.reshape(ORDER, z.slice, width),
        gain_two.reshape(z.slice),
        gate_grad,
        up_grad,
        down_grad.T,
    )


def solution(mesh):
    placed = (
        P("dp", None, None),
        P("dp", None, None),
        P("dp"),
        P(),
        P(),
        P(),
        P(None, "tensor", None, None),
        P(),
        P(),
        P(None, "tensor"),
        P(None, "tensor"),
        P("tensor", None),
    )
    return jax.shard_map(
        functools.partial(body, dict(mesh.shape)),
        mesh=mesh,
        in_specs=placed,
        out_specs=(
            P("dp", None, None),
            P("dp", None, None),
            P("dp"),
            P(None, "tensor", "dp", None),
            P(None, "dp", None),
            P("dp"),
            P("dp", "tensor"),
            P("dp", "tensor"),
            P("tensor", "dp"),
        ),
        check_vma=False,
    )
```

```python
import functools

import jax
import jax.numpy as jnp
from jax import lax
from jax.experimental import pallas as pl
from jax.experimental.pallas import tpu as pltpu
from jax.sharding import PartitionSpec as P

F32 = jnp.float32
BF16 = jnp.bfloat16
MESH = pl.DeviceIdType.MESH
EPSILON = 1e-06
ROOT_HALF = 0.7071067811865476
INV_ROOT_TWO_PI = 0.3989422804014327
ORDER = 3
MIB = 2**20


def dot(left, right):
    return jnp.dot(left, right, preferred_element_type=F32)


def dot_cols(left, right):
    return lax.dot_general(left, right, (((1,), (1,)), ((), ())), preferred_element_type=F32)


def dot_rows(left, right):
    return lax.dot_general(left, right, (((0,), (0,)), ((), ())), preferred_element_type=F32)


def rms_scale(values):
    return lax.rsqrt(jnp.mean(values * values, axis=-1, keepdims=True) + EPSILON)


def row_sign(rows):
    odd = lax.broadcasted_iota(jnp.int32, (rows, 1), 0) % 2
    return 1.0 - 2.0 * odd.astype(F32)


def lane_sign(lanes):
    odd = lax.broadcasted_iota(jnp.int32, (1, lanes), 1) % 2
    return 1.0 - 2.0 * odd.astype(F32)


def aligned(index, step):
    return pl.ds(pl.multiple_of(index * step, step), step)


class Sizes:
    def __init__(self, mesh_shape, inputs, mixer_weights, filters, w_gate):
        self.seqs, self.length, self.width = inputs
        self.rows = self.seqs * self.length
        self.dp = mesh_shape["dp"]
        self.tensor = mesh_shape["tensor"]
        self.line = self.dp // 4
        self.own = mixer_weights[1]
        self.filters = filters[0]
        self.hidden = w_gate[1]
        self.slice = self.width // self.dp
        self.group = max(g for g in range(1, 5) if self.own % g == 0)
        self.depth = self.group * self.width
        self.chunks = 2 * self.own // self.group
        self.half = self.width // 2
        self.near = self.dp // 2 * self.length
        self.pair_rows = 2 * self.own * self.slice
        self.ar_rows = ORDER * self.slice
        self.all_rows = 2 * self.pair_rows + self.ar_rows


def place(z):
    dp = lax.axis_index("dp")
    return dp // 4, (dp // 2) % 2, dp % 2, lax.axis_index("tensor")


def dp_of(line, side, core):
    return (line * 2 + side) * 2 + core


def reversed_rows(filters_ref):
    length = filters_ref.shape[1]
    source = lax.broadcasted_iota(jnp.int32, (length, length), 0)
    target = lax.broadcasted_iota(jnp.int32, (length, length), 1)
    pick = (source == (length + length // 2 - target) % length).astype(BF16)
    return dot(filters_ref[...], pick)


def toeplitz_own(z, own_first, rows_ref, out_ref):
    length, half = z.length, z.length // 2
    lane = lax.broadcasted_iota(jnp.int32, (half, length), 1)
    row = lax.broadcasted_iota(jnp.int32, (half, length), 0)

    def step(k, carry):
        values = jnp.broadcast_to(rows_ref[pl.ds(own_first + k, 1), :], (half, length))
        rolled = pltpu.roll(values, 0, 1, stride=1, stride_axis=0)
        lower = jnp.where(lane <= row + half, rolled, 0.0).astype(BF16)
        out_ref[k, half:, :] = lower
        out_ref[k, :half, :half] = lower[:, half:]
        out_ref[k, :half, half:] = jnp.zeros((half, half), BF16)
        return carry

    lax.fori_loop(0, z.own, step, 0)


def shared_copy(buffer, slot, send, recv, peer):
    return pltpu.make_async_remote_copy(
        src_ref=buffer.at[slot],
        dst_ref=buffer.at[slot],
        send_sem=send,
        recv_sem=recv,
        device_id=(lax.axis_index("dp"), peer),
        device_id_type=MESH,
    )


class Exchange:
    def __init__(self, z, buffer, send, recv):
        self.z, self.buffer, self.send, self.recv = z, buffer, send, recv

    def copies(self, part):
        me = lax.axis_index("tensor")
        return [
            shared_copy(
                self.buffer.at[part],
                me,
                self.send.at[part, step - 1],
                self.recv.at[part, step - 1],
                (me + step) % self.z.tensor,
            )
            for step in range(1, self.z.tensor)
        ]

    def start(self, part):
        for copy in self.copies(part):
            copy.start()

    def wait(self, part):
        for copy in self.copies(part):
            copy.wait()

    def total(self, part, where):
        terms = [self.buffer[(part, peer) + where].astype(F32) for peer in range(self.z.tensor)]
        return functools.reduce(jnp.add, terms)


def block_kernel(
    z,
    ids_ref,
    group_ref,
    x_ref,
    cotangent_ref,
    filters_ref,
    gain_one_ref,
    gain_two_ref,
    mixer_hbm,
    ar_hbm,
    gate_hbm,
    up_hbm,
    down_hbm,
    output_hbm,
    input_grad_hbm,
    mixer_grad_hbm,
    ar_grad_hbm,
    weight_grad_hbm,
    gain_grad_hbm,
    output_ref,
    input_grad_ref,
    ar_grad_ref,
    weight_grad_ref,
    gain_grad_ref,
    mixer_ref,
    ar_ref,
    gate_ref,
    up_ref,
    down_ref,
    signed_ref,
    lagged_ref,
    turned_mine,
    turned_ref,
    signed_turned,
    taps_ref,
    rows_ref,
    plain_rows_ref,
    toeplitz_ref,
    conv_ref,
    conv_near,
    sum_ref,
    normed_two_ref,
    low_ref,
    active_ref,
    gate_pre_ref,
    up_pre_ref,
    mixed_ref,
    mixed_turned,
    grad_conv_ref,
    back_ref,
    ar_back_ref,
    gathered,
    part_one,
    part_two,
    part_three,
    part_out,
    pair_send,
    pair_recv,
    grads_ref,
    ring_core,
    ring_side,
    ring_line,
    gains,
    mixer_sem,
    load_sem,
    write_sem,
    turn_own,
    turn_send,
    turn_recv,
    one_send,
    one_recv,
    two_send,
    two_recv,
    three_send,
    three_recv,
    out_send,
    out_recv,
    gather_send,
    gather_side_send,
    gather_recv,
    core_send,
    core_recv,
    side_send,
    side_recv,
    line_send,
    line_recv,
    pair_send_sem,
    pair_recv_sem,
    gain_send,
    gain_recv,
):
    line, side, core, across = place(z)
    me = lax.axis_index("dp")
    length, width, rows, half = z.length, z.width, z.rows, z.half
    lines, own, steps = z.line, z.own, z.own // z.group
    other = dp_of(line, side, 1 - core)
    opposite = dp_of(line, 1 - side, core)
    partner = across + 1 - 2 * (across % 2)
    own_seq = (across + core) % 2

    def mixer_load(q):
        slot = q % 3
        source = mixer_hbm.at[aligned(q % z.chunks, z.depth), :]
        return pltpu.make_async_copy(source, mixer_ref.at[slot], mixer_sem.at[slot])

    loads = [
        pltpu.make_async_copy(source, target, load_sem.at[index])
        for index, (source, target) in enumerate(
            ((ar_hbm, ar_ref), (gate_hbm, gate_ref), (up_hbm, up_ref), (down_hbm, down_ref))
        )
    ]
    mixer_load(0).start()
    mixer_load(1).start()
    mixer_load(2).start()

    barrier = pltpu.get_barrier_semaphore()
    for step in range(1, z.tensor):
        pl.semaphore_signal(barrier, inc=1, device_id=(me, (across + step) % z.tensor), device_id_type=MESH)
    for step in range(1, z.dp):
        pl.semaphore_signal(barrier, inc=1, device_id=((me + step) % z.dp, across), device_id_type=MESH)

    sign = row_sign(length)
    turned_sign = lane_sign(length)
    for seq in range(z.seqs):
        values = x_ref[seq * length : (seq + 1) * length, :].astype(F32)
        normed = (values * rms_scale(values) * gain_one_ref[...]).astype(BF16)
        signed_ref[seq, :, :width] = normed
        signed_ref[seq, :, width:] = (normed.astype(F32) * sign).astype(BF16)
    rows_ref[...] = reversed_rows(filters_ref)
    plain_rows_ref[...] = filters_ref[...].astype(F32)
    toeplitz_own(z, across * own, rows_ref, toeplitz_ref)

    exchange_one = Exchange(z, part_one, one_send, one_recv)
    exchange_two = Exchange(z, part_two, two_send, two_recv)
    exchange_three = Exchange(z, part_three, three_send, three_recv)
    exchange_out = Exchange(z, part_out, out_send, out_recv)

    def seq_rows(seq):
        return slice(seq * length, (seq + 1) * length)

    def mix(seq):
        def convolve(k, carry):
            result = dot(toeplitz_ref[k], signed_ref[seq]).astype(BF16)
            for j in range(2):
                chunk = j * steps + k // z.group
                conv_near[aligned(chunk, length), aligned(k % z.group, width)] = result[:, j * width : (j + 1) * width]
            return carry

        lax.fori_loop(0, own, convolve, 0, unroll=3)
        if seq == 0:
            for load in loads:
                load.start()
        sum_ref[: 2 * length, :] = jnp.zeros((2 * length, width), F32)

        def project(i, carry):
            q = seq * z.chunks + i
            mixer_load(q).wait()
            sum_ref[aligned(i // steps, length), :] += dot(conv_near[aligned(i, length), : z.depth], mixer_ref[q % 3])
            mixer_load(q + 3).start()
            return carry

        lax.fori_loop(0, z.chunks, project, 0, unroll=2)
        part_one[seq, across] = (sum_ref[:length, :] + sign * sum_ref[length : 2 * length, :]).astype(BF16)

    mix(0)
    pl.semaphore_wait(barrier, z.dp - 1 + z.tensor - 1)
    exchange_one.start(0)

    turned_mine[...] = signed_ref[own_seq, :, :width].astype(F32).T.astype(BF16).reshape(z.dp, z.slice, length)

    def turn_copy(step):
        peer = (me + step) % z.dp
        far = (side + (peer // 2) % 2) % 2
        return pltpu.make_async_remote_copy(
            src_ref=turned_mine.at[peer],
            dst_ref=turned_ref.at[far * (2 * lines) + line * 2 + core],
            send_sem=turn_send.at[step - 1],
            recv_sem=turn_recv.at[step - 1],
            device_id=(peer, across),
            device_id_type=MESH,
        )

    for step in range(1, z.dp):
        turn_copy(step).start()
    turn_mine = pltpu.make_async_copy(turned_mine.at[me], turned_ref.at[line * 2 + core], turn_own)
    turn_mine.start()

    mix(1)
    exchange_one.start(1)

    row = lax.broadcasted_iota(jnp.int32, (length, 1), 0)
    loads[0].wait()
    scales = []
    for seq in range(z.seqs):
        own_rows = seq_rows(seq)
        normed = signed_ref[seq, :, :width].astype(F32)
        for lag in range(ORDER):
            shifted = jnp.where(row >= lag, pltpu.roll(normed, lag, 0), 0.0) if lag else normed
            lagged_ref[own_rows, lag * width : (lag + 1) * width] = shifted.astype(BF16)
        scale = jnp.int32(0)
        for group in range(group_ref.shape[0]):
            scale = scale + jnp.where(ids_ref[seq] == group, group_ref[group], 0)
        scales.append(scale.astype(F32))
        low_ref[own_rows, :] = (cotangent_ref[own_rows, :].astype(F32) * scales[seq]).astype(BF16)
    output_ref[...] = dot(lagged_ref[...], ar_ref[...])

    chunk = min(256, z.hidden)

    def feed_forward(seq):
        own_rows = seq_rows(seq)
        exchange_one.wait(seq)
        for start in range(seq * length, (seq + 1) * length, 128):
            block = slice(start, start + 128)
            inside = slice(start - seq * length, start - seq * length + 128)
            hidden = x_ref[block, :].astype(F32) + (exchange_one.total(seq, (inside,)) + output_ref[block, :])
            output_ref[block, :] = hidden
            normed_two_ref[block, :] = (hidden * rms_scale(hidden) * gain_two_ref[...]).astype(BF16)
        if seq == 0:
            for load in loads[1:]:
                load.wait()

        def feed(c, carry):
            units = aligned(c, chunk)
            gate = dot(normed_two_ref[own_rows, :], gate_ref[:, units])
            up = dot(normed_two_ref[own_rows, :], up_ref[:, units])
            cdf = 0.5 * (1.0 + lax.erf(gate * ROOT_HALF))
            activated = gate * cdf
            active_ref[own_rows, units] = (activated * up).astype(BF16)
            grad = dot_cols(low_ref[own_rows, :], down_ref[units, :])
            density = jnp.exp(-0.5 * gate * gate) * INV_ROOT_TWO_PI
            gate_pre_ref[own_rows, units] = (grad * up * (cdf + gate * density)).astype(BF16)
            up_pre_ref[own_rows, units] = (grad * activated).astype(BF16)
            return carry

        lax.fori_loop(0, z.hidden // chunk, feed, 0)
        grad = dot_cols(gate_pre_ref[own_rows, :], gate_ref[...]) + dot_cols(up_pre_ref[own_rows, :], up_ref[...])
        part_two[seq, across] = grad.astype(BF16)
        exchange_two.start(seq)

    for seq in range(z.seqs):
        feed_forward(seq)

    def core_copy(index):
        return pltpu.make_async_remote_copy(
            src_ref=grads_ref.at[index, :, :, 1 - core],
            dst_ref=ring_core.at[index],
            send_sem=core_send.at[index],
            recv_sem=core_recv.at[index],
            device_id=(other, across),
            device_id_type=MESH,
        )

    for index, (left, right) in enumerate(
        ((normed_two_ref, gate_pre_ref), (normed_two_ref, up_pre_ref), (low_ref, active_ref))
    ):
        product = dot_rows(left[...], right[...]).astype(BF16)
        grads_ref[index] = product.reshape(lines, 2, 2, z.slice, z.hidden)
        core_copy(index).start()
    for seq in range(z.seqs):
        part_out[seq, across] = dot(active_ref[seq_rows(seq), :], down_ref[...]).astype(BF16)

    def slot_of(far, at):
        return far * (2 * lines) + at * 2 + core

    def gather_copy(part, source, target, send, peer):
        return pltpu.make_async_remote_copy(
            src_ref=gathered.at[part, aligned(source, length), :],
            dst_ref=gathered.at[part, aligned(target, length), :],
            send_sem=send,
            recv_sem=gather_recv.at[part, target],
            device_id=(peer, across),
            device_id_type=MESH,
        )

    def line_block(part, away, up):
        at = line - away if up else line + away
        slot = slot_of(0, at)
        sems = gather_send.at[part, away, up]
        onward = dp_of(jnp.clip(line + (1 if up else -1), 0, lines - 1), side, core)
        return (
            jnp.logical_and(at >= 0, at < lines),
            lambda: gather_copy(part, slot, slot_of(1, at), sems.at[0], opposite),
            lambda: gather_copy(part, slot, slot, sems.at[1], other),
            lambda: gather_copy(part, slot, slot, sems.at[2], onward),
        )

    def has_onward(up):
        return line + 1 < lines if up else line >= 1

    def start_copy(copy):
        copy.start()

    def finish_copy(copy):
        copy.wait_send()

    def line_round(part, away, act):
        if away == 0:
            _, to_side, to_core, to_line = line_block(part, 0, 1)
            _, _, _, down_line = line_block(part, 0, 0)
            pl.when(has_onward(1))(lambda: act(to_line()))
            pl.when(has_onward(0))(lambda: act(down_line()))
            act(to_side())
            act(to_core())
            return
        for up in (1, 0):
            there, to_side, to_core, to_line = line_block(part, away, up)

            def pass_on(to_side=to_side, to_core=to_core, to_line=to_line, up=up):
                if act is start_copy:
                    to_core().wait_recv()
                pl.when(has_onward(up))(lambda: act(to_line()))
                act(to_side())
                act(to_core())

            pl.when(there)(pass_on)

    def side_round(part, away, act):
        for up in (1, 0) if away else (1,):
            at = line - away if up else line + away

            def pass_on(at=at, up=up):
                slot = slot_of(1, at)
                copy = gather_copy(part, slot, slot, gather_side_send.at[part, away, up], other)
                if act is start_copy:
                    copy.wait_recv()
                act(copy)

            pl.when(jnp.logical_and(at >= 0, at < lines))(pass_on)

    def await_core(part, far):
        for at in range(lines):
            slot = far * (2 * lines) + at * 2 + 1 - core
            gather_copy(part, slot, slot, gather_side_send.at[part, 0, 0], other).wait_recv()

    def mixed_gradient(seq):
        exchange_two.wait(seq)
        gain = jnp.zeros((1, width), F32)
        for start in range(seq * length, (seq + 1) * length, 128):
            block = slice(start, start + 128)
            inside = slice(start - seq * length, start - seq * length + 128)
            grad = exchange_two.total(seq, (inside,))
            hidden = output_ref[block, :]
            scale = rms_scale(hidden)
            normed = hidden * scale
            gain = gain + jnp.sum(grad * normed, axis=0, keepdims=True)
            weighted = grad * gain_two_ref[...]
            upstream = cotangent_ref[block, :].astype(F32) * scales[seq]
            grad_hidden = upstream + scale * (weighted - normed * jnp.mean(weighted * normed, axis=-1, keepdims=True))
            input_grad_ref[block, :] = grad_hidden
            mixed_ref[block, :] = grad_hidden.astype(BF16)

        def send():
            for part in range(2):
                gathered[part, aligned(slot_of(0, line), length), :] = mixed_ref[
                    seq_rows(seq), part * half : (part + 1) * half
                ]
            line_round(0, 0, start_copy)

        pl.when(own_seq == seq)(send)
        return gain

    def side_copy(index):
        return pltpu.make_async_remote_copy(
            src_ref=grads_ref.at[index, :, 1 - side, core],
            dst_ref=ring_side.at[index],
            send_sem=side_send.at[index],
            recv_sem=side_recv.at[index],
            device_id=(opposite, across),
            device_id_type=MESH,
        )

    def reduce_core(index):
        core_copy(index).wait()
        for at in range(lines):
            for where in range(2):
                grads_ref[index, at, where, core] = (
                    grads_ref[index, at, where, core].astype(F32) + ring_core[index, at, where].astype(F32)
                ).astype(BF16)
        side_copy(index).start()

    def line_copy(index, step):
        target = (line + step) % lines
        return pltpu.make_async_remote_copy(
            src_ref=ring_side.at[index, target],
            dst_ref=ring_line.at[index, step - 1],
            send_sem=line_send.at[index, step - 1],
            recv_sem=line_recv.at[index, step - 1],
            device_id=(dp_of(target, side, core), across),
            device_id_type=MESH,
        )

    def reduce_side(index):
        side_copy(index).wait()
        for at in range(lines):
            ring_side[index, at] = (
                ring_side[index, at].astype(F32) + grads_ref[index, at, side, core].astype(F32)
            ).astype(BF16)
        for step in range(1, lines):
            line_copy(index, step).start()

    def write(source, target, index):
        copy = pltpu.make_async_copy(source, target, write_sem.at[index])
        copy.start()
        return copy

    second = 4 + z.chunks + 2
    positions = second + z.chunks + 2
    plan = {at: [] for at in range(positions)}

    def at_position(at, last, event, *args):
        plan[min(at, last)].append(functools.partial(event, *args))

    for late in range(2):

        def when_own(event, *args, late=late):
            pl.when(own_seq == late)(functools.partial(event, *args))

        first = 4 * late
        for part in range(2):
            last = (second - 3, positions - 3)[part]
            if part:
                at_position(first + 1, last, when_own, line_round, part, 0, start_copy)
            for away in range(1, lines):
                at_position(first + 2 * part + away - 1, last, when_own, line_round, part, away, start_copy)
                at_position(first + 2 * part + away, last, when_own, side_round, part, away - 1, start_copy)
            at_position(first + 2 * part + lines, last, when_own, side_round, part, lines - 1, start_copy)
    for index in range(3):
        at_position(second - 4 + index, positions - 1, reduce_core, index)
        at_position(second + 2 + 2 * index, positions - 1, reduce_side, index)

    def poll(at):
        for event in plan[at]:
            event()

    gain_two = mixed_gradient(0)
    lane = lax.broadcasted_iota(jnp.int32, (1, length), 1)

    for step in range(1, z.dp):
        turn_copy(step).wait()
    turn_mine.wait()
    slots = z.dp
    for slot in range(slots):
        own_rows = slice(slot * z.slice, (slot + 1) * z.slice)
        normed = turned_ref[slot].astype(F32)
        signed_turned[own_rows, :] = turned_ref[slot]
        signed_turned[pl.ds(z.dp * z.slice + slot * z.slice, z.slice), :] = (normed * turned_sign).astype(BF16)
        conv = (conv_ref, conv_near)[slot // (2 * lines)]
        cols = slice(slot % (2 * lines) * length, (slot % (2 * lines) + 1) * length)
        for lag in range(ORDER):
            shifted = jnp.where(lane >= lag, pltpu.roll(normed, lag, 1), 0.0) if lag else normed
            at = 2 * z.pair_rows + lag * z.slice
            conv[at : at + z.slice, cols] = shifted.astype(BF16)
    half_length = length // 2
    tap_row = lax.broadcasted_iota(jnp.int32, (half_length, length), 0)
    tap_lane = lax.broadcasted_iota(jnp.int32, (half_length, length), 1)

    def build_taps(k, carry):
        values = jnp.broadcast_to(plain_rows_ref[pl.ds((across - across % 2) * own + k, 1), :], (half_length, length))
        upper = jnp.where(tap_lane >= tap_row, pltpu.roll(values, 0, 1, stride=1, stride_axis=0), 0.0)
        lower = jnp.concatenate([jnp.zeros((half_length, half_length), F32), upper[:, :half_length]], axis=1)
        taps_ref[k] = jnp.concatenate([upper, lower], axis=0).astype(BF16)
        return carry

    lax.fori_loop(0, 2 * own, build_taps, 0, unroll=2)
    signed_rows = z.dp * z.slice

    def convolve_slice(k, carry):
        both = dot(signed_turned[...], taps_ref[k])
        first = (k // own) * z.pair_rows + (k % own) * z.slice
        for j in range(2):
            result = both[j * signed_rows : (j + 1) * signed_rows, :]
            if j:
                result = result * turned_sign
            result = result.astype(BF16)
            at = pl.ds(pl.multiple_of(first + j * own * z.slice, z.slice), z.slice)
            for slot in range(slots):
                conv = (conv_ref, conv_near)[slot // (2 * lines)]
                cols = slice(slot % (2 * lines) * length, (slot % (2 * lines) + 1) * length)
                conv[at, cols] = result[slot * z.slice : (slot + 1) * z.slice, :]
        return carry

    for quarter in range(4):
        lax.fori_loop(quarter * 2 * own // 4, (quarter + 1) * 2 * own // 4, convolve_slice, 0, unroll=2)
        poll(quarter)
        if quarter == 1:
            gain_two = gain_two + mixed_gradient(1)
            for seq in range(z.seqs):
                exchange_out.start(seq)

    def back(seq):
        turned = mixed_ref[seq_rows(seq), :].astype(F32).T
        mixed_turned[0] = turned.astype(BF16)
        mixed_turned[1] = (turned * turned_sign).astype(BF16)
        for i in range(z.chunks):
            q = (2 + seq) * z.chunks + i
            j, g = i // steps, i % steps
            mixer_load(q).wait()

            def project(k, carry):
                result = dot(mixer_ref[q % 3, aligned(k, width), :], mixed_turned[j]).astype(BF16)
                grad_conv_ref[:, aligned(k, length)] = result
                return carry

            lax.fori_loop(0, z.group, project, 0, unroll=True)
            if q + 3 < 4 * z.chunks:
                mixer_load(q + 3).start()
            taps = toeplitz_ref[g * z.group : (g + 1) * z.group].reshape(z.group * length, length)
            product = dot(grad_conv_ref[...], taps)
            back_ref[j] = product if g == 0 else back_ref[j] + product
            poll((4, second)[seq] + i)
        part_three[seq, across] = (back_ref[0] + turned_sign * back_ref[1]).astype(BF16)
        exchange_three.start(seq)

    def pair_copy(part):
        return pltpu.make_async_remote_copy(
            src_ref=pair_send.at[part],
            dst_ref=pair_recv.at[part],
            send_sem=pair_send_sem.at[part],
            recv_sem=pair_recv_sem.at[part],
            device_id=(me, partner),
            device_id_type=MESH,
        )

    mine, theirs = aligned(across % 2, z.pair_rows), aligned(1 - across % 2, z.pair_rows)
    shared = slice(2 * z.pair_rows, z.all_rows)
    for part in range(2):
        back(part)
        cols = slice(part * half, (part + 1) * half)

        def add_product(taken, far, cols=cols, part=part):
            tokens = slice(far * z.near, (far + 1) * z.near)
            product = dot((conv_ref, conv_near)[far][taken, : z.near], gathered[part, tokens, :])
            sum_ref[taken, cols] = product if far == 0 else sum_ref[taken, cols] + product

        await_core(part, 0)
        for taken in (mine, theirs, shared):
            add_product(taken, 0)
        poll((second, positions)[part] - 2)
        await_core(part, 1)
        for taken in (theirs, shared):
            add_product(taken, 1)
        pair_send[part, : z.pair_rows, :] = sum_ref[theirs, cols].astype(BF16)
        pair_send[part, z.pair_rows :, :] = sum_ref[shared, cols].astype(BF16)
        pair_copy(part).start()
        add_product(mine, 1)
        poll((second, positions)[part] - 1)

    for seq in range(z.seqs):
        turned = mixed_ref[seq_rows(seq), :].astype(F32).T
        total = dot(ar_ref[:width, :], turned.astype(BF16))
        for lag in range(1, ORDER):
            shifted = jnp.where(lane < length - lag, pltpu.roll(turned, length - lag, 1), 0.0).astype(BF16)
            total = total + dot(ar_ref[lag * width : (lag + 1) * width, :], shifted)
        ar_back_ref[seq] = total
    for seq in range(z.seqs):
        exchange_out.wait(seq)
        output_ref[seq_rows(seq), :] += exchange_out.total(seq, ())
    writes = [write(output_ref, output_hbm, 1)]

    gain_one = jnp.zeros((1, width), F32)
    for seq in range(z.seqs):
        exchange_three.wait(seq)
        grad = (exchange_three.total(seq, ()) + ar_back_ref[seq]).T
        own_rows = seq_rows(seq)
        values = x_ref[own_rows, :].astype(F32)
        scale = rms_scale(values)
        normed = values * scale
        gain_one = gain_one + jnp.sum(grad * normed, axis=0, keepdims=True)
        weighted = grad * gain_one_ref[...]
        input_grad_ref[own_rows, :] += scale * (
            weighted - normed * jnp.mean(weighted * normed, axis=-1, keepdims=True)
        )
    gains[me] = jnp.concatenate([gain_two, gain_one], axis=0)

    def gain_copy(step):
        return pltpu.make_async_remote_copy(
            src_ref=gains.at[me],
            dst_ref=gains.at[me],
            send_sem=gain_send.at[step - 1],
            recv_sem=gain_recv.at[step - 1],
            device_id=((me + step) % z.dp, across),
            device_id_type=MESH,
        )

    for step in range(1, z.dp):
        gain_copy(step).start()
    writes.append(write(input_grad_ref, input_grad_hbm, 0))

    for index in range(3):
        total = ring_side[index, line].astype(F32)
        for step in range(1, lines):
            line_copy(index, step).wait()
            total = total + ring_line[index, step - 1].astype(F32)
        weight_grad_ref[index] = total
    writes.append(write(weight_grad_ref, weight_grad_hbm, 2))

    for step in range(1, z.dp):
        gain_copy(step).wait()
    gain_grad_ref[...] = functools.reduce(jnp.add, [gains[index] for index in range(z.dp)])
    writes.append(write(gain_grad_ref, gain_grad_hbm, 3))

    for part in range(2):
        cols = slice(part * half, (part + 1) * half)
        pair_copy(part).wait()
        sum_ref[mine, cols] += pair_recv[part, : z.pair_rows, :].astype(F32)
        ar_grad_ref[:, cols] = pair_send[part, z.pair_rows :, :].astype(F32) + pair_recv[
            part, z.pair_rows :, :
        ].astype(F32)
    writes.append(write(sum_ref.at[mine, :], mixer_grad_hbm, 4))
    writes.append(write(ar_grad_ref, ar_grad_hbm, 5))

    for part in range(2):
        for away in range(lines):
            line_round(part, away, finish_copy)
            side_round(part, away, finish_copy)
    for copy in writes:
        copy.wait()


def finish_kernel(z, gains_ref, *refs):
    sources, targets, (gain_one_out, gain_two_out) = refs[:5], refs[5:12], refs[12:14]
    held, (read_sem, write_sem) = refs[14:19], refs[19:]
    reads = [pltpu.make_async_copy(*pair, read_sem.at[index]) for index, pair in enumerate(zip(sources, held))]
    for read in reads:
        read.start()
    first = lax.axis_index("dp") * z.slice
    rolled = pltpu.roll(gains_ref[...], (z.width - first) % z.width, 1)
    gain_two_out[...] = rolled[0:1, : z.slice]
    gain_one_out[...] = rolled[1:2, : z.slice]
    parts = [*held[:4], *(held[4].at[index] for index in range(3))]
    writes = [pltpu.make_async_copy(*pair, write_sem.at[index]) for index, pair in enumerate(zip(parts, targets))]
    for index, write in enumerate(writes):
        if index < len(reads):
            reads[index].wait()
        write.start()
    for write in writes:
        write.wait()


VMEM_SPEC = pl.BlockSpec(memory_space=pltpu.VMEM)
HBM_SPEC = pl.BlockSpec(memory_space=pl.ANY)
SMEM_SPEC = pl.BlockSpec(memory_space=pltpu.SMEM)
DMA = pltpu.SemaphoreType.DMA


def shape(dims, dtype=F32):
    return jax.ShapeDtypeStruct(dims, dtype)


def low(*dims):
    return pltpu.VMEM(dims, BF16)


def wide(*dims):
    return pltpu.VMEM(dims, F32)


def body(
    mesh_shape,
    inputs,
    cotangent,
    group_ids,
    group_weights,
    filters,
    gain_mixer,
    mixer_weights,
    ar_weights,
    gain_mlp,
    w_gate,
    w_up,
    w_down,
):
    z = Sizes(mesh_shape, inputs.shape, mixer_weights.shape, filters.T.shape, w_gate.shape)
    length, width, rows, half, lines = z.length, z.width, z.rows, z.half, z.line
    others, far_lines = z.tensor - 1, max(1, lines - 1)
    grads = (
        shape((rows, width)),
        shape((rows, width)),
        shape((z.pair_rows, width)),
        shape((z.ar_rows, width)),
        shape((3, z.slice, z.hidden)),
    )
    output, input_grad, mixer_grad, ar_grad, weight_grads, gains = pl.pallas_call(
        functools.partial(block_kernel, z),
        name="block",
        out_shape=(*grads, shape((2, width))),
        in_specs=[SMEM_SPEC] * 2 + [VMEM_SPEC] * 5 + [HBM_SPEC] * 5,
        out_specs=(HBM_SPEC,) * 6,
        scratch_shapes=[
            wide(rows, width),
            wide(rows, width),
            wide(z.ar_rows, width),
            wide(3, z.slice, z.hidden),
            wide(2, width),
            low(3, z.depth, width),
            low(ORDER * width, width),
            low(width, z.hidden),
            low(width, z.hidden),
            low(z.hidden, width),
            low(z.seqs, length, 2 * width),
            low(rows, ORDER * width),
            low(z.dp, z.slice, length),
            low(z.dp, z.slice, length),
            low(2 * z.dp * z.slice, length),
            low(2 * z.own, length, length),
            wide(z.filters, length),
            wide(z.filters, length),
            low(z.own, length, length),
            low(z.all_rows, z.near),
            low(max(z.all_rows, z.chunks * length), max(z.near, z.depth)),
            wide(max(z.all_rows, 2 * length), width),
            low(rows, width),
            low(rows, width),
            low(rows, z.hidden),
            low(rows, z.hidden),
            low(rows, z.hidden),
            low(rows, width),
            low(2, width, length),
            low(width, z.group * length),
            wide(2, width, length),
            wide(z.seqs, width, length),
            low(2, z.dp * length, half),
            low(z.seqs, z.tensor, length, width),
            low(z.seqs, z.tensor, length, width),
            low(z.seqs, z.tensor, width, length),
            low(z.seqs, z.tensor, length, width),
            low(2, z.pair_rows + z.ar_rows, half),
            low(2, z.pair_rows + z.ar_rows, half),
            low(3, lines, 2, 2, z.slice, z.hidden),
            low(3, lines, 2, z.slice, z.hidden),
            low(3, lines, z.slice, z.hidden),
            low(3, far_lines, z.slice, z.hidden),
            wide(z.dp, 2, width),
            DMA((3,)),
            DMA((4,)),
            DMA((6,)),
            DMA,
            DMA((z.dp - 1,)),
            DMA((z.dp - 1,)),
            *[DMA((z.seqs, others))] * 8,
            DMA((2, lines, 2, 3)),
            DMA((2, lines, 2)),
            DMA((2, z.dp)),
            *[DMA((3,))] * 4,
            DMA((3, far_lines)),
            DMA((3, far_lines)),
            DMA((2,)),
            DMA((2,)),
            DMA((z.dp - 1,)),
            DMA((z.dp - 1,)),
        ],
        compiler_params=pltpu.CompilerParams(collective_id=1, has_side_effects=True, vmem_limit_bytes=63 * MIB),
    )(
        group_ids,
        group_weights,
        inputs.reshape(rows, width),
        cotangent.reshape(rows, width),
        filters.T,
        gain_mixer.reshape(1, width),
        gain_mlp.reshape(1, width),
        mixer_weights.reshape(2 * z.own * width, width),
        ar_weights.reshape(ORDER * width, width),
        w_gate,
        w_up,
        w_down,
    )
    (
        output,
        input_grad,
        mixer_grad,
        ar_grad,
        gate_grad,
        up_grad,
        down_grad,
        gain_one,
        gain_two,
    ) = pl.pallas_call(
        functools.partial(finish_kernel, z),
        name="finish",
        out_shape=(*grads[:4], *[shape((z.slice, z.hidden))] * 3, *[shape((1, z.slice))] * 2),
        in_specs=[VMEM_SPEC] + [HBM_SPEC] * 5,
        out_specs=(HBM_SPEC,) * 7 + (VMEM_SPEC,) * 2,
        scratch_shapes=[*[pltpu.VMEM(grad.shape, F32) for grad in grads], DMA((5,)), DMA((7,))],
    )(gains, output, input_grad, mixer_grad, ar_grad, weight_grads)
    return (
        output.reshape(inputs.shape),
        input_grad.reshape(inputs.shape),
        gain_one.reshape(z.slice),
        mixer_grad.reshape(2, z.own, z.slice, width),
        ar_grad.reshape(ORDER, z.slice, width),
        gain_two.reshape(z.slice),
        gate_grad,
        up_grad,
        down_grad.T,
    )


def solution(mesh):
    placed = (
        P("dp", None, None),
        P("dp", None, None),
        P("dp"),
        P(),
        P(),
        P(),
        P(None, "tensor", None, None),
        P(),
        P(),
        P(None, "tensor"),
        P(None, "tensor"),
        P("tensor", None),
    )
    return jax.shard_map(
        functools.partial(body, dict(mesh.shape)),
        mesh=mesh,
        in_specs=placed,
        out_specs=(
            P("dp", None, None),
            P("dp", None, None),
            P("dp"),
            P(None, "tensor", "dp", None),
            P(None, "dp", None),
            P("dp"),
            P("dp", "tensor"),
            P("dp", "tensor"),
            P("tensor", "dp"),
        ),
        check_vma=False,
    )
```

```python
import functools

import jax
import jax.numpy as jnp
from jax import lax
from jax.experimental import pallas as pl
from jax.experimental.pallas import tpu as pltpu
from jax.sharding import PartitionSpec as P

F32 = jnp.float32
BF16 = jnp.bfloat16
MESH = pl.DeviceIdType.MESH
EPSILON = 1e-06
ROOT_HALF = 0.7071067811865476
INV_ROOT_TWO_PI = 0.3989422804014327
ORDER = 3
MIB = 2**20


def dot(left, right):
    return jnp.dot(left, right, preferred_element_type=F32)


def dot_cols(left, right):
    return lax.dot_general(left, right, (((1,), (1,)), ((), ())), preferred_element_type=F32)


def dot_rows(left, right):
    return lax.dot_general(left, right, (((0,), (0,)), ((), ())), preferred_element_type=F32)


def rms_scale(values):
    return lax.rsqrt(jnp.mean(values * values, axis=-1, keepdims=True) + EPSILON)


def row_sign(rows):
    odd = lax.broadcasted_iota(jnp.int32, (rows, 1), 0) % 2
    return 1.0 - 2.0 * odd.astype(F32)


def lane_sign(lanes):
    odd = lax.broadcasted_iota(jnp.int32, (1, lanes), 1) % 2
    return 1.0 - 2.0 * odd.astype(F32)


def aligned(index, step):
    return pl.ds(pl.multiple_of(index * step, step), step)


class Sizes:
    def __init__(self, mesh_shape, inputs, mixer_weights, filters, w_gate):
        self.seqs, self.length, self.width = inputs
        self.rows = self.seqs * self.length
        self.dp = mesh_shape["dp"]
        self.tensor = mesh_shape["tensor"]
        self.line = self.dp // 4
        self.own = mixer_weights[1]
        self.filters = filters[0]
        self.hidden = w_gate[1]
        self.slice = self.width // self.dp
        self.group = max(g for g in range(1, 5) if self.own % g == 0)
        self.depth = self.group * self.width
        self.chunks = 2 * self.own // self.group
        self.half = self.width // 2
        self.near = self.dp // 2 * self.length
        self.pair_rows = 2 * self.own * self.slice
        self.ar_rows = ORDER * self.slice
        self.all_rows = 2 * self.pair_rows + self.ar_rows


def place(z):
    dp = lax.axis_index("dp")
    return dp // 4, (dp // 2) % 2, dp % 2, lax.axis_index("tensor")


def dp_of(line, side, core):
    return (line * 2 + side) * 2 + core


def reversed_rows(filters_ref):
    length = filters_ref.shape[1]
    source = lax.broadcasted_iota(jnp.int32, (length, length), 0)
    target = lax.broadcasted_iota(jnp.int32, (length, length), 1)
    pick = (source == (length + length // 2 - target) % length).astype(BF16)
    return dot(filters_ref[...], pick)


def toeplitz_own(z, own_first, rows_ref, out_ref):
    length, half = z.length, z.length // 2
    lane = lax.broadcasted_iota(jnp.int32, (half, length), 1)
    row = lax.broadcasted_iota(jnp.int32, (half, length), 0)

    def step(k, carry):
        values = jnp.broadcast_to(rows_ref[pl.ds(own_first + k, 1), :], (half, length))
        rolled = pltpu.roll(values, 0, 1, stride=1, stride_axis=0)
        lower = jnp.where(lane <= row + half, rolled, 0.0).astype(BF16)
        out_ref[k, half:, :] = lower
        out_ref[k, :half, :half] = lower[:, half:]
        out_ref[k, :half, half:] = jnp.zeros((half, half), BF16)
        return carry

    lax.fori_loop(0, z.own, step, 0)


def shared_copy(buffer, slot, send, recv, peer):
    return pltpu.make_async_remote_copy(
        src_ref=buffer.at[slot],
        dst_ref=buffer.at[slot],
        send_sem=send,
        recv_sem=recv,
        device_id=(lax.axis_index("dp"), peer),
        device_id_type=MESH,
    )


class Exchange:
    def __init__(self, z, buffer, send, recv):
        self.z, self.buffer, self.send, self.recv = z, buffer, send, recv

    def copies(self, part):
        me = lax.axis_index("tensor")
        return [
            shared_copy(
                self.buffer.at[part],
                me,
                self.send.at[part, step - 1],
                self.recv.at[part, step - 1],
                (me + step) % self.z.tensor,
            )
            for step in range(1, self.z.tensor)
        ]

    def start(self, part):
        for copy in self.copies(part):
            copy.start()

    def wait(self, part):
        for copy in self.copies(part):
            copy.wait()

    def total(self, part, where):
        terms = [self.buffer[(part, peer) + where].astype(F32) for peer in range(self.z.tensor)]
        return functools.reduce(jnp.add, terms)


def block_kernel(
    z,
    ids_ref,
    group_ref,
    x_ref,
    cotangent_ref,
    filters_ref,
    gain_one_ref,
    gain_two_ref,
    mixer_hbm,
    ar_hbm,
    gate_hbm,
    up_hbm,
    down_hbm,
    output_hbm,
    input_grad_hbm,
    mixer_grad_hbm,
    ar_grad_hbm,
    weight_grad_hbm,
    gain_grad_hbm,
    output_ref,
    input_grad_ref,
    ar_grad_ref,
    weight_grad_ref,
    gain_grad_ref,
    mixer_ref,
    ar_ref,
    gate_ref,
    up_ref,
    down_ref,
    signed_ref,
    lagged_ref,
    turned_mine,
    turned_ref,
    signed_turned,
    taps_ref,
    rows_ref,
    plain_rows_ref,
    toeplitz_ref,
    conv_ref,
    conv_near,
    sum_ref,
    normed_two_ref,
    low_ref,
    active_ref,
    gate_pre_ref,
    up_pre_ref,
    mixed_ref,
    mixed_turned,
    grad_conv_ref,
    back_ref,
    ar_back_ref,
    gathered,
    part_one,
    part_two,
    part_three,
    part_out,
    pair_send,
    pair_recv,
    grads_ref,
    ring_core,
    ring_side,
    ring_line,
    gains,
    mixer_sem,
    load_sem,
    write_sem,
    turn_own,
    turn_send,
    turn_recv,
    one_send,
    one_recv,
    two_send,
    two_recv,
    three_send,
    three_recv,
    out_send,
    out_recv,
    gather_send,
    gather_side_send,
    gather_recv,
    core_send,
    core_recv,
    side_send,
    side_recv,
    line_send,
    line_recv,
    pair_send_sem,
    pair_recv_sem,
    gain_send,
    gain_recv,
):
    line, side, core, across = place(z)
    me = lax.axis_index("dp")
    length, width, rows, half = z.length, z.width, z.rows, z.half
    lines, own, steps = z.line, z.own, z.own // z.group
    other = dp_of(line, side, 1 - core)
    opposite = dp_of(line, 1 - side, core)
    partner = across + 1 - 2 * (across % 2)
    own_seq = (across + core) % 2

    def mixer_load(q):
        slot = q % 3
        source = mixer_hbm.at[aligned(q % z.chunks, z.depth), :]
        return pltpu.make_async_copy(source, mixer_ref.at[slot], mixer_sem.at[slot])

    loads = [
        pltpu.make_async_copy(source, target, load_sem.at[index])
        for index, (source, target) in enumerate(
            ((ar_hbm, ar_ref), (gate_hbm, gate_ref), (up_hbm, up_ref), (down_hbm, down_ref))
        )
    ]
    mixer_load(0).start()
    mixer_load(1).start()
    mixer_load(2).start()

    barrier = pltpu.get_barrier_semaphore()
    for step in range(1, z.tensor):
        pl.semaphore_signal(barrier, inc=1, device_id=(me, (across + step) % z.tensor), device_id_type=MESH)
    for step in range(1, z.dp):
        pl.semaphore_signal(barrier, inc=1, device_id=((me + step) % z.dp, across), device_id_type=MESH)

    sign = row_sign(length)
    turned_sign = lane_sign(length)
    for seq in range(z.seqs):
        values = x_ref[seq * length : (seq + 1) * length, :].astype(F32)
        normed = (values * rms_scale(values) * gain_one_ref[...]).astype(BF16)
        signed_ref[seq, :, :width] = normed
        signed_ref[seq, :, width:] = (normed.astype(F32) * sign).astype(BF16)
    rows_ref[...] = reversed_rows(filters_ref)
    plain_rows_ref[...] = filters_ref[...].astype(F32)
    toeplitz_own(z, across * own, rows_ref, toeplitz_ref)

    exchange_one = Exchange(z, part_one, one_send, one_recv)
    exchange_two = Exchange(z, part_two, two_send, two_recv)
    exchange_three = Exchange(z, part_three, three_send, three_recv)
    exchange_out = Exchange(z, part_out, out_send, out_recv)

    def seq_rows(seq):
        return slice(seq * length, (seq + 1) * length)

    def mix(seq):
        def convolve(k, carry):
            result = dot(toeplitz_ref[k], signed_ref[seq]).astype(BF16)
            for j in range(2):
                chunk = j * steps + k // z.group
                conv_near[aligned(chunk, length), aligned(k % z.group, width)] = result[:, j * width : (j + 1) * width]
            return carry

        lax.fori_loop(0, own, convolve, 0, unroll=3)
        if seq == 0:
            for load in loads:
                load.start()
        sum_ref[: 2 * length, :] = jnp.zeros((2 * length, width), F32)

        def project(i, carry):
            q = seq * z.chunks + i
            mixer_load(q).wait()
            sum_ref[aligned(i // steps, length), :] += dot(conv_near[aligned(i, length), : z.depth], mixer_ref[q % 3])
            mixer_load(q + 3).start()
            return carry

        lax.fori_loop(0, z.chunks, project, 0, unroll=2)
        part_one[seq, across] = (sum_ref[:length, :] + sign * sum_ref[length : 2 * length, :]).astype(BF16)

    mix(0)
    pl.semaphore_wait(barrier, z.dp - 1 + z.tensor - 1)
    exchange_one.start(0)

    turned_mine[...] = signed_ref[own_seq, :, :width].astype(F32).T.astype(BF16).reshape(z.dp, z.slice, length)

    def turn_copy(step):
        peer = (me + step) % z.dp
        far = (side + (peer // 2) % 2) % 2
        return pltpu.make_async_remote_copy(
            src_ref=turned_mine.at[peer],
            dst_ref=turned_ref.at[far * (2 * lines) + line * 2 + core],
            send_sem=turn_send.at[step - 1],
            recv_sem=turn_recv.at[step - 1],
            device_id=(peer, across),
            device_id_type=MESH,
        )

    for step in range(1, z.dp):
        turn_copy(step).start()
    turn_mine = pltpu.make_async_copy(turned_mine.at[me], turned_ref.at[line * 2 + core], turn_own)
    turn_mine.start()

    mix(1)
    exchange_one.start(1)

    row = lax.broadcasted_iota(jnp.int32, (length, 1), 0)
    loads[0].wait()
    scales = []
    for seq in range(z.seqs):
        own_rows = seq_rows(seq)
        normed = signed_ref[seq, :, :width].astype(F32)
        for lag in range(ORDER):
            shifted = jnp.where(row >= lag, pltpu.roll(normed, lag, 0), 0.0) if lag else normed
            lagged_ref[own_rows, lag * width : (lag + 1) * width] = shifted.astype(BF16)
        scale = jnp.int32(0)
        for group in range(group_ref.shape[0]):
            scale = scale + jnp.where(ids_ref[seq] == group, group_ref[group], 0)
        scales.append(scale.astype(F32))
        low_ref[own_rows, :] = (cotangent_ref[own_rows, :].astype(F32) * scales[seq]).astype(BF16)
    output_ref[...] = dot(lagged_ref[...], ar_ref[...])

    chunk = min(256, z.hidden)

    def feed_forward(seq):
        own_rows = seq_rows(seq)
        exchange_one.wait(seq)
        for start in range(seq * length, (seq + 1) * length, 128):
            block = slice(start, start + 128)
            inside = slice(start - seq * length, start - seq * length + 128)
            hidden = x_ref[block, :].astype(F32) + (exchange_one.total(seq, (inside,)) + output_ref[block, :])
            output_ref[block, :] = hidden
            normed_two_ref[block, :] = (hidden * rms_scale(hidden) * gain_two_ref[...]).astype(BF16)
        if seq == 0:
            for load in loads[1:]:
                load.wait()

        def feed(c, carry):
            units = aligned(c, chunk)
            gate = dot(normed_two_ref[own_rows, :], gate_ref[:, units])
            up = dot(normed_two_ref[own_rows, :], up_ref[:, units])
            cdf = 0.5 * (1.0 + lax.erf(gate * ROOT_HALF))
            activated = gate * cdf
            active_ref[own_rows, units] = (activated * up).astype(BF16)
            grad = dot_cols(low_ref[own_rows, :], down_ref[units, :])
            density = jnp.exp(-0.5 * gate * gate) * INV_ROOT_TWO_PI
            gate_pre_ref[own_rows, units] = (grad * up * (cdf + gate * density)).astype(BF16)
            up_pre_ref[own_rows, units] = (grad * activated).astype(BF16)
            return carry

        lax.fori_loop(0, z.hidden // chunk, feed, 0)
        grad = dot_cols(gate_pre_ref[own_rows, :], gate_ref[...]) + dot_cols(up_pre_ref[own_rows, :], up_ref[...])
        part_two[seq, across] = grad.astype(BF16)
        exchange_two.start(seq)

    for seq in range(z.seqs):
        feed_forward(seq)

    def core_copy(index):
        return pltpu.make_async_remote_copy(
            src_ref=grads_ref.at[index, :, :, 1 - core],
            dst_ref=ring_core.at[index],
            send_sem=core_send.at[index],
            recv_sem=core_recv.at[index],
            device_id=(other, across),
            device_id_type=MESH,
        )

    for index, (left, right) in enumerate(
        ((normed_two_ref, gate_pre_ref), (normed_two_ref, up_pre_ref), (low_ref, active_ref))
    ):
        product = dot_rows(left[...], right[...]).astype(BF16)
        grads_ref[index] = product.reshape(lines, 2, 2, z.slice, z.hidden)
        core_copy(index).start()
    for seq in range(z.seqs):
        part_out[seq, across] = dot(active_ref[seq_rows(seq), :], down_ref[...]).astype(BF16)

    def slot_of(far, at):
        return far * (2 * lines) + at * 2 + core

    def gather_copy(part, source, target, send, peer):
        return pltpu.make_async_remote_copy(
            src_ref=gathered.at[part, aligned(source, length), :],
            dst_ref=gathered.at[part, aligned(target, length), :],
            send_sem=send,
            recv_sem=gather_recv.at[part, target],
            device_id=(peer, across),
            device_id_type=MESH,
        )

    def line_block(part, away, up):
        at = line - away if up else line + away
        slot = slot_of(0, at)
        sems = gather_send.at[part, away, up]
        onward = dp_of(jnp.clip(line + (1 if up else -1), 0, lines - 1), side, core)
        return (
            jnp.logical_and(at >= 0, at < lines),
            lambda: gather_copy(part, slot, slot_of(1, at), sems.at[0], opposite),
            lambda: gather_copy(part, slot, slot, sems.at[1], other),
            lambda: gather_copy(part, slot, slot, sems.at[2], onward),
        )

    def has_onward(up):
        return line + 1 < lines if up else line >= 1

    def start_copy(copy):
        copy.start()

    def finish_copy(copy):
        copy.wait_send()

    def line_round(part, away, act):
        if away == 0:
            _, to_side, to_core, to_line = line_block(part, 0, 1)
            _, _, _, down_line = line_block(part, 0, 0)
            pl.when(has_onward(1))(lambda: act(to_line()))
            pl.when(has_onward(0))(lambda: act(down_line()))
            act(to_side())
            act(to_core())
            return
        for up in (1, 0):
            there, to_side, to_core, to_line = line_block(part, away, up)

            def pass_on(to_side=to_side, to_core=to_core, to_line=to_line, up=up):
                if act is start_copy:
                    to_core().wait_recv()
                pl.when(has_onward(up))(lambda: act(to_line()))
                act(to_side())
                act(to_core())

            pl.when(there)(pass_on)

    def side_round(part, away, act):
        for up in (1, 0) if away else (1,):
            at = line - away if up else line + away

            def pass_on(at=at, up=up):
                slot = slot_of(1, at)
                copy = gather_copy(part, slot, slot, gather_side_send.at[part, away, up], other)
                if act is start_copy:
                    copy.wait_recv()
                act(copy)

            pl.when(jnp.logical_and(at >= 0, at < lines))(pass_on)

    def await_core(part, far):
        for at in range(lines):
            slot = far * (2 * lines) + at * 2 + 1 - core
            gather_copy(part, slot, slot, gather_side_send.at[part, 0, 0], other).wait_recv()

    def mixed_gradient(seq):
        exchange_two.wait(seq)
        gain = jnp.zeros((1, width), F32)
        for start in range(seq * length, (seq + 1) * length, 128):
            block = slice(start, start + 128)
            inside = slice(start - seq * length, start - seq * length + 128)
            grad = exchange_two.total(seq, (inside,))
            hidden = output_ref[block, :]
            scale = rms_scale(hidden)
            normed = hidden * scale
            gain = gain + jnp.sum(grad * normed, axis=0, keepdims=True)
            weighted = grad * gain_two_ref[...]
            upstream = cotangent_ref[block, :].astype(F32) * scales[seq]
            grad_hidden = upstream + scale * (weighted - normed * jnp.mean(weighted * normed, axis=-1, keepdims=True))
            input_grad_ref[block, :] = grad_hidden
            mixed_ref[block, :] = grad_hidden.astype(BF16)

        def send():
            for part in range(2):
                gathered[part, aligned(slot_of(0, line), length), :] = mixed_ref[
                    seq_rows(seq), part * half : (part + 1) * half
                ]
            line_round(0, 0, start_copy)

        pl.when(own_seq == seq)(send)
        return gain

    def side_copy(index):
        return pltpu.make_async_remote_copy(
            src_ref=grads_ref.at[index, :, 1 - side, core],
            dst_ref=ring_side.at[index],
            send_sem=side_send.at[index],
            recv_sem=side_recv.at[index],
            device_id=(opposite, across),
            device_id_type=MESH,
        )

    def reduce_core(index):
        core_copy(index).wait()
        for at in range(lines):
            for where in range(2):
                grads_ref[index, at, where, core] = (
                    grads_ref[index, at, where, core].astype(F32) + ring_core[index, at, where].astype(F32)
                ).astype(BF16)
        side_copy(index).start()

    def line_copy(index, step):
        target = (line + step) % lines
        return pltpu.make_async_remote_copy(
            src_ref=ring_side.at[index, target],
            dst_ref=ring_line.at[index, step - 1],
            send_sem=line_send.at[index, step - 1],
            recv_sem=line_recv.at[index, step - 1],
            device_id=(dp_of(target, side, core), across),
            device_id_type=MESH,
        )

    def reduce_side(index):
        side_copy(index).wait()
        for at in range(lines):
            ring_side[index, at] = (
                ring_side[index, at].astype(F32) + grads_ref[index, at, side, core].astype(F32)
            ).astype(BF16)
        for step in range(1, lines):
            line_copy(index, step).start()

    def write(source, target, index):
        copy = pltpu.make_async_copy(source, target, write_sem.at[index])
        copy.start()
        return copy

    second = 4 + z.chunks + 2
    positions = second + z.chunks + 2
    plan = {at: [] for at in range(positions)}

    def at_position(at, last, event, *args):
        plan[min(at, last)].append(functools.partial(event, *args))

    for late in range(2):

        def when_own(event, *args, late=late):
            pl.when(own_seq == late)(functools.partial(event, *args))

        first = 4 * late
        for part in range(2):
            last = (second - 3, positions - 3)[part]
            if part:
                at_position(first + 1, last, when_own, line_round, part, 0, start_copy)
            for away in range(1, lines):
                at_position(first + 2 * part + away - 1, last, when_own, line_round, part, away, start_copy)
                at_position(first + 2 * part + away, last, when_own, side_round, part, away - 1, start_copy)
            at_position(first + 2 * part + lines, last, when_own, side_round, part, lines - 1, start_copy)
    for index in range(3):
        at_position(second - 4 + index, positions - 1, reduce_core, index)
        at_position(second + 2 + 2 * index, positions - 1, reduce_side, index)

    def poll(at):
        for event in plan[at]:
            event()

    gain_two = mixed_gradient(0)
    lane = lax.broadcasted_iota(jnp.int32, (1, length), 1)

    for step in range(1, z.dp):
        turn_copy(step).wait()
    turn_mine.wait()
    slots = z.dp
    for slot in range(slots):
        own_rows = slice(slot * z.slice, (slot + 1) * z.slice)
        normed = turned_ref[slot].astype(F32)
        signed_turned[own_rows, :] = turned_ref[slot]
        signed_turned[pl.ds(z.dp * z.slice + slot * z.slice, z.slice), :] = (normed * turned_sign).astype(BF16)
        conv = (conv_ref, conv_near)[slot // (2 * lines)]
        cols = slice(slot % (2 * lines) * length, (slot % (2 * lines) + 1) * length)
        for lag in range(ORDER):
            shifted = jnp.where(lane >= lag, pltpu.roll(normed, lag, 1), 0.0) if lag else normed
            at = 2 * z.pair_rows + lag * z.slice
            conv[at : at + z.slice, cols] = shifted.astype(BF16)
    half_length = length // 2
    tap_row = lax.broadcasted_iota(jnp.int32, (half_length, length), 0)
    tap_lane = lax.broadcasted_iota(jnp.int32, (half_length, length), 1)

    def build_taps(k, carry):
        values = jnp.broadcast_to(plain_rows_ref[pl.ds((across - across % 2) * own + k, 1), :], (half_length, length))
        upper = jnp.where(tap_lane >= tap_row, pltpu.roll(values, 0, 1, stride=1, stride_axis=0), 0.0)
        lower = jnp.concatenate([jnp.zeros((half_length, half_length), F32), upper[:, :half_length]], axis=1)
        taps_ref[k] = jnp.concatenate([upper, lower], axis=0).astype(BF16)
        return carry

    lax.fori_loop(0, 2 * own, build_taps, 0, unroll=2)
    signed_rows = z.dp * z.slice

    def convolve_slice(k, carry):
        both = dot(signed_turned[...], taps_ref[k])
        first = (k // own) * z.pair_rows + (k % own) * z.slice
        for j in range(2):
            result = both[j * signed_rows : (j + 1) * signed_rows, :]
            if j:
                result = result * turned_sign
            result = result.astype(BF16)
            at = pl.ds(pl.multiple_of(first + j * own * z.slice, z.slice), z.slice)
            for slot in range(slots):
                conv = (conv_ref, conv_near)[slot // (2 * lines)]
                cols = slice(slot % (2 * lines) * length, (slot % (2 * lines) + 1) * length)
                conv[at, cols] = result[slot * z.slice : (slot + 1) * z.slice, :]
        return carry

    for quarter in range(4):
        lax.fori_loop(quarter * 2 * own // 4, (quarter + 1) * 2 * own // 4, convolve_slice, 0, unroll=2)
        poll(quarter)
        if quarter == 1:
            gain_two = gain_two + mixed_gradient(1)
            for seq in range(z.seqs):
                exchange_out.start(seq)

    def back(seq):
        turned = mixed_ref[seq_rows(seq), :].astype(F32).T
        mixed_turned[0] = turned.astype(BF16)
        mixed_turned[1] = (turned * turned_sign).astype(BF16)
        for i in range(z.chunks):
            q = (2 + seq) * z.chunks + i
            j, g = i // steps, i % steps
            mixer_load(q).wait()

            def project(k, carry):
                result = dot(mixer_ref[q % 3, aligned(k, width), :], mixed_turned[j]).astype(BF16)
                grad_conv_ref[:, aligned(k, length)] = result
                return carry

            lax.fori_loop(0, z.group, project, 0, unroll=True)
            if q + 3 < 4 * z.chunks:
                mixer_load(q + 3).start()
            taps = toeplitz_ref[g * z.group : (g + 1) * z.group].reshape(z.group * length, length)
            product = dot(grad_conv_ref[...], taps)
            back_ref[j] = product if g == 0 else back_ref[j] + product
            poll((4, second)[seq] + i)
        part_three[seq, across] = (back_ref[0] + turned_sign * back_ref[1]).astype(BF16)
        exchange_three.start(seq)

    def pair_copy(part):
        return pltpu.make_async_remote_copy(
            src_ref=pair_send.at[part],
            dst_ref=pair_recv.at[part],
            send_sem=pair_send_sem.at[part],
            recv_sem=pair_recv_sem.at[part],
            device_id=(me, partner),
            device_id_type=MESH,
        )

    mine, theirs = aligned(across % 2, z.pair_rows), aligned(1 - across % 2, z.pair_rows)
    shared = slice(2 * z.pair_rows, z.all_rows)
    for part in range(2):
        back(part)
        cols = slice(part * half, (part + 1) * half)

        def add_product(taken, far, cols=cols, part=part):
            tokens = slice(far * z.near, (far + 1) * z.near)
            product = dot((conv_ref, conv_near)[far][taken, : z.near], gathered[part, tokens, :])
            sum_ref[taken, cols] = product if far == 0 else sum_ref[taken, cols] + product

        await_core(part, 0)
        for taken in (mine, theirs, shared):
            add_product(taken, 0)
        poll((second, positions)[part] - 2)
        await_core(part, 1)
        for taken in (theirs, shared):
            add_product(taken, 1)
        pair_send[part, : z.pair_rows, :] = sum_ref[theirs, cols].astype(BF16)
        pair_send[part, z.pair_rows :, :] = sum_ref[shared, cols].astype(BF16)
        pair_copy(part).start()
        add_product(mine, 1)
        poll((second, positions)[part] - 1)

    for seq in range(z.seqs):
        turned = mixed_ref[seq_rows(seq), :].astype(F32).T
        total = dot(ar_ref[:width, :], turned.astype(BF16))
        for lag in range(1, ORDER):
            shifted = jnp.where(lane < length - lag, pltpu.roll(turned, length - lag, 1), 0.0).astype(BF16)
            total = total + dot(ar_ref[lag * width : (lag + 1) * width, :], shifted)
        ar_back_ref[seq] = total
    for seq in range(z.seqs):
        exchange_out.wait(seq)
        output_ref[seq_rows(seq), :] += exchange_out.total(seq, ())
    writes = [write(output_ref, output_hbm, 1)]

    gain_one = jnp.zeros((1, width), F32)
    for seq in range(z.seqs):
        exchange_three.wait(seq)
        grad = (exchange_three.total(seq, ()) + ar_back_ref[seq]).T
        own_rows = seq_rows(seq)
        values = x_ref[own_rows, :].astype(F32)
        scale = rms_scale(values)
        normed = values * scale
        gain_one = gain_one + jnp.sum(grad * normed, axis=0, keepdims=True)
        weighted = grad * gain_one_ref[...]
        input_grad_ref[own_rows, :] += scale * (
            weighted - normed * jnp.mean(weighted * normed, axis=-1, keepdims=True)
        )
    gains[me] = jnp.concatenate([gain_two, gain_one], axis=0)

    def gain_copy(step):
        return pltpu.make_async_remote_copy(
            src_ref=gains.at[me],
            dst_ref=gains.at[me],
            send_sem=gain_send.at[step - 1],
            recv_sem=gain_recv.at[step - 1],
            device_id=((me + step) % z.dp, across),
            device_id_type=MESH,
        )

    for step in range(1, z.dp):
        gain_copy(step).start()
    writes.append(write(input_grad_ref, input_grad_hbm, 0))

    for index in range(3):
        total = ring_side[index, line].astype(F32)
        for step in range(1, lines):
            line_copy(index, step).wait()
            total = total + ring_line[index, step - 1].astype(F32)
        weight_grad_ref[index] = total
    writes.append(write(weight_grad_ref, weight_grad_hbm, 2))

    for step in range(1, z.dp):
        gain_copy(step).wait()
    gain_grad_ref[...] = functools.reduce(jnp.add, [gains[index] for index in range(z.dp)])
    writes.append(write(gain_grad_ref, gain_grad_hbm, 3))

    for part in range(2):
        for away in range(lines):
            line_round(part, away, finish_copy)
            side_round(part, away, finish_copy)
    for part in range(2):
        cols = slice(part * half, (part + 1) * half)
        pair_copy(part).wait()
        sum_ref[mine, cols] += pair_recv[part, : z.pair_rows, :].astype(F32)
        writes.append(write(sum_ref.at[mine, cols], mixer_grad_hbm.at[:, cols], 4 + part))
        ar_grad_ref[:, cols] = pair_send[part, z.pair_rows :, :].astype(F32) + pair_recv[
            part, z.pair_rows :, :
        ].astype(F32)
    writes.append(write(ar_grad_ref, ar_grad_hbm, 6))

    for copy in writes:
        copy.wait()


def finish_kernel(z, gains_ref, *refs):
    sources, targets, (gain_one_out, gain_two_out) = refs[:5], refs[5:12], refs[12:14]
    held, (read_sem, write_sem) = refs[14:19], refs[19:]
    reads = [pltpu.make_async_copy(*pair, read_sem.at[index]) for index, pair in enumerate(zip(sources, held))]
    for read in reads:
        read.start()
    first = lax.axis_index("dp") * z.slice
    rolled = pltpu.roll(gains_ref[...], (z.width - first) % z.width, 1)
    gain_two_out[...] = rolled[0:1, : z.slice]
    gain_one_out[...] = rolled[1:2, : z.slice]
    parts = [*held[:4], *(held[4].at[index] for index in range(3))]
    writes = [pltpu.make_async_copy(*pair, write_sem.at[index]) for index, pair in enumerate(zip(parts, targets))]
    for index, write in enumerate(writes):
        if index < len(reads):
            reads[index].wait()
        write.start()
    for write in writes:
        write.wait()


VMEM_SPEC = pl.BlockSpec(memory_space=pltpu.VMEM)
HBM_SPEC = pl.BlockSpec(memory_space=pl.ANY)
SMEM_SPEC = pl.BlockSpec(memory_space=pltpu.SMEM)
DMA = pltpu.SemaphoreType.DMA


def shape(dims, dtype=F32):
    return jax.ShapeDtypeStruct(dims, dtype)


def low(*dims):
    return pltpu.VMEM(dims, BF16)


def wide(*dims):
    return pltpu.VMEM(dims, F32)


def body(
    mesh_shape,
    inputs,
    cotangent,
    group_ids,
    group_weights,
    filters,
    gain_mixer,
    mixer_weights,
    ar_weights,
    gain_mlp,
    w_gate,
    w_up,
    w_down,
):
    z = Sizes(mesh_shape, inputs.shape, mixer_weights.shape, filters.T.shape, w_gate.shape)
    length, width, rows, half, lines = z.length, z.width, z.rows, z.half, z.line
    others, far_lines = z.tensor - 1, max(1, lines - 1)
    grads = (
        shape((rows, width)),
        shape((rows, width)),
        shape((z.pair_rows, width)),
        shape((z.ar_rows, width)),
        shape((3, z.slice, z.hidden)),
    )
    output, input_grad, mixer_grad, ar_grad, weight_grads, gains = pl.pallas_call(
        functools.partial(block_kernel, z),
        name="block",
        out_shape=(*grads, shape((2, width))),
        in_specs=[SMEM_SPEC] * 2 + [VMEM_SPEC] * 5 + [HBM_SPEC] * 5,
        out_specs=(HBM_SPEC,) * 6,
        scratch_shapes=[
            wide(rows, width),
            wide(rows, width),
            wide(z.ar_rows, width),
            wide(3, z.slice, z.hidden),
            wide(2, width),
            low(3, z.depth, width),
            low(ORDER * width, width),
            low(width, z.hidden),
            low(width, z.hidden),
            low(z.hidden, width),
            low(z.seqs, length, 2 * width),
            low(rows, ORDER * width),
            low(z.dp, z.slice, length),
            low(z.dp, z.slice, length),
            low(2 * z.dp * z.slice, length),
            low(2 * z.own, length, length),
            wide(z.filters, length),
            wide(z.filters, length),
            low(z.own, length, length),
            low(z.all_rows, z.near),
            low(max(z.all_rows, z.chunks * length), max(z.near, z.depth)),
            wide(max(z.all_rows, 2 * length), width),
            low(rows, width),
            low(rows, width),
            low(rows, z.hidden),
            low(rows, z.hidden),
            low(rows, z.hidden),
            low(rows, width),
            low(2, width, length),
            low(width, z.group * length),
            wide(2, width, length),
            wide(z.seqs, width, length),
            low(2, z.dp * length, half),
            low(z.seqs, z.tensor, length, width),
            low(z.seqs, z.tensor, length, width),
            low(z.seqs, z.tensor, width, length),
            low(z.seqs, z.tensor, length, width),
            low(2, z.pair_rows + z.ar_rows, half),
            low(2, z.pair_rows + z.ar_rows, half),
            low(3, lines, 2, 2, z.slice, z.hidden),
            low(3, lines, 2, z.slice, z.hidden),
            low(3, lines, z.slice, z.hidden),
            low(3, far_lines, z.slice, z.hidden),
            wide(z.dp, 2, width),
            DMA((3,)),
            DMA((4,)),
            DMA((7,)),
            DMA,
            DMA((z.dp - 1,)),
            DMA((z.dp - 1,)),
            *[DMA((z.seqs, others))] * 8,
            DMA((2, lines, 2, 3)),
            DMA((2, lines, 2)),
            DMA((2, z.dp)),
            *[DMA((3,))] * 4,
            DMA((3, far_lines)),
            DMA((3, far_lines)),
            DMA((2,)),
            DMA((2,)),
            DMA((z.dp - 1,)),
            DMA((z.dp - 1,)),
        ],
        compiler_params=pltpu.CompilerParams(collective_id=1, has_side_effects=True, vmem_limit_bytes=63 * MIB),
    )(
        group_ids,
        group_weights,
        inputs.reshape(rows, width),
        cotangent.reshape(rows, width),
        filters.T,
        gain_mixer.reshape(1, width),
        gain_mlp.reshape(1, width),
        mixer_weights.reshape(2 * z.own * width, width),
        ar_weights.reshape(ORDER * width, width),
        w_gate,
        w_up,
        w_down,
    )
    (
        output,
        input_grad,
        mixer_grad,
        ar_grad,
        gate_grad,
        up_grad,
        down_grad,
        gain_one,
        gain_two,
    ) = pl.pallas_call(
        functools.partial(finish_kernel, z),
        name="finish",
        out_shape=(*grads[:4], *[shape((z.slice, z.hidden))] * 3, *[shape((1, z.slice))] * 2),
        in_specs=[VMEM_SPEC] + [HBM_SPEC] * 5,
        out_specs=(HBM_SPEC,) * 7 + (VMEM_SPEC,) * 2,
        scratch_shapes=[*[pltpu.VMEM(grad.shape, F32) for grad in grads], DMA((5,)), DMA((7,))],
    )(gains, output, input_grad, mixer_grad, ar_grad, weight_grads)
    return (
        output.reshape(inputs.shape),
        input_grad.reshape(inputs.shape),
        gain_one.reshape(z.slice),
        mixer_grad.reshape(2, z.own, z.slice, width),
        ar_grad.reshape(ORDER, z.slice, width),
        gain_two.reshape(z.slice),
        gate_grad,
        up_grad,
        down_grad.T,
    )


def solution(mesh):
    placed = (
        P("dp", None, None),
        P("dp", None, None),
        P("dp"),
        P(),
        P(),
        P(),
        P(None, "tensor", None, None),
        P(),
        P(),
        P(None, "tensor"),
        P(None, "tensor"),
        P("tensor", None),
    )
    return jax.shard_map(
        functools.partial(body, dict(mesh.shape)),
        mesh=mesh,
        in_specs=placed,
        out_specs=(
            P("dp", None, None),
            P("dp", None, None),
            P("dp"),
            P(None, "tensor", "dp", None),
            P(None, "dp", None),
            P("dp"),
            P("dp", "tensor"),
            P("dp", "tensor"),
            P("tensor", "dp"),
        ),
        check_vma=False,
    )
```
